256 devices in a mesh: row: 32 (over z_hi, x, core), col: 8 (over z_lo, y).
Axes of the slice: x: 4, y: 4, z: 8 (z_hi: 4, z_lo: 2; z = z_hi * 2 + z_lo), core: 2. Of those that a mesh axis runs over, the one named last changes fastest.
Arguments:
- mask: float32 [4096, 1024], P('row', 'col'), may hold values from 0 to 1
- mask_prev: float32 [4096, 1024], P('row', 'col'), may hold values from 0 to 1
- target: float32 [4096, 1024], P('row', 'col'), may hold values from 0 to 1
- kernels: float32 [8, 2, 129, 129], replicated, may hold values from -0.01953125 to 0.01953125
- restart: int32 [2, 32, 8], P(None, 'row', 'col'), may hold values from 0 to 1
Outputs:
- mask_next: float32 [4096, 1024], P('row', 'col')
- mask_last: float32 [4096, 1024], P('row', 'col')
- objective: float32 [2], replicated
The draws below stay inside these ranges and needn't reach their ends.
All inputs are finite; a program needn't handle non-finite values.
Results may differ from the reference program's by a relative error of at most 0.0001.
Values sent between devices are 32-bit elements; how exact they have to be, the bound alone decides.
A program may use at most 128 MiB of HBM per device.

```python
import jax
import jax.numpy as jnp
from jax import lax

TR = 128
TC = 128
KS = 129
KERNELS = 8
ITERS = 2
NX = 4096
NY = 1024
TILES_R = 32
TILES_C = 8


def place_ends(drawn, key, least, largest):
    place = [jax.random.randint(jax.random.fold_in(key, axis), (), 0, length) for axis, length in enumerate(drawn.shape)]
    widest = drawn.shape.index(max(drawn.shape))
    beside = place[:widest] + [(place[widest] + 1) % drawn.shape[widest]] + place[widest + 1:]
    return drawn.at[tuple(place)].set(least).at[tuple(beside)].set(largest)


def block_levels(stream_key, extent, cuts, low, top_value):
    loudness = 1.0
    for axis_at, blocks in cuts:
        draws = jax.random.uniform(jax.random.fold_in(jax.random.fold_in(stream_key, 6), axis_at), (blocks,), jnp.float32, low / len(cuts), top_value / len(cuts))
        loudness = loudness * jnp.repeat(jnp.exp(draws), extent[axis_at] // blocks).reshape((-1,) + (1,) * (len(extent) - 1 - axis_at))
    return loudness


def normal_values(own_key, extent, scale, most, kind=jnp.bfloat16):
    return jnp.clip(scale * jax.random.normal(own_key, extent, jnp.float32), -most, most).astype(kind)


def setup_inputs(seed: int = 0) -> dict:
    key_of = jax.random.split(jax.random.key(seed), 6)
    return {
        "mask": jnp.clip(1.0 * jax.random.uniform(key_of[0], (NX, NY), jnp.float32) ** block_levels(key_of[0], (NX, NY), ((0, 32), (1, 8)), -0.2, 0.2), 0.0, 1.0),
        "mask_prev": jnp.clip(1.0 * jax.random.uniform(key_of[1], (NX, NY), jnp.float32) ** block_levels(key_of[1], (NX, NY), ((0, 32), (1, 8)), -0.2, 0.2), 0.0, 1.0),
        "target": jnp.clip(1.0 * jax.random.uniform(key_of[2], (NX, NY), jnp.float32) ** block_levels(key_of[2], (NX, NY), ((0, 32), (1, 8)), -0.2, 0.2), 0.0, 1.0),
        "kernels": normal_values(key_of[3], (KERNELS, 2, KS, KS), (3 * KS * KS * KERNELS // 4) ** -0.5, 0.01953125, jnp.float32),
        "restart": place_ends(jax.random.randint(key_of[4], (ITERS, TILES_R, TILES_C), 0, 2), jax.random.fold_in(key_of[4], 1), 0, 1).astype(jnp.int32),
    }


SLOPE = 4.0
LEVEL = 0.8
STEP_SIZE = 0.05
TV_WEIGHT = 0.05
L1_WEIGHT = 0.5
EPS_TV = 0.01
PRIOR_STEPS = 10.0

def kernel_spectra(real_part, imag_part, len_rows, len_cols):
    radius = (KS - 1) // 2
    placed_real = jnp.zeros((KERNELS, len_rows, len_cols), jnp.float32).at[:, :KS, :KS].set(real_part)
    placed_imag = jnp.zeros((KERNELS, len_rows, len_cols), jnp.float32).at[:, :KS, :KS].set(imag_part)
    placed = lax.complex(placed_real, placed_imag)
    placed = jnp.roll(placed, (-radius, -radius), axis=(1, 2))
    return jnp.fft.fft2(placed, axes=(1, 2))

def reference(mask, mask_prev, target, kernels, restart):
    radius = (KS - 1) // 2
    len_rows = NX + 2 * radius
    len_cols = NY + 2 * radius
    kernel_real = kernels[:, 0]
    kernel_imag = kernels[:, 1]
    forward_spectrum = kernel_spectra(kernel_real[:, ::-1, ::-1], kernel_imag[:, ::-1, ::-1], len_rows, len_cols)
    adjoint_spectrum = kernel_spectra(kernel_real, -kernel_imag, len_rows, len_cols)
    current = mask
    previous = mask_prev
    totals = []
    for iteration in range(ITERS):
        momentum = (iteration + PRIOR_STEPS - 1.0) / (iteration + PRIOR_STEPS + 2.0)
        flags = jnp.repeat(jnp.repeat(restart[iteration], TR, axis=0), TC, axis=1)
        keep_share = 1.0 - flags.astype(mask.dtype)
        extrapolated = current + keep_share * momentum * (current - previous)
        spread = jnp.fft.fft2(jnp.pad(extrapolated, ((0, 2 * radius), (0, 2 * radius))))
        image_field = jnp.fft.ifft2(spread[None] * forward_spectrum, axes=(1, 2))[:, :NX, :NY]
        field_real = jnp.real(image_field)
        field_imag = jnp.imag(image_field)
        intensity = lax.optimization_barrier(jnp.sum(field_real * field_real + field_imag * field_imag, axis=0))
        resist = jax.nn.sigmoid(SLOPE * (intensity - LEVEL))
        weight = 2.0 * (resist - target) * SLOPE * resist * (1.0 - resist)
        sources = lax.complex(weight * field_real, weight * field_imag)
        sources = jnp.pad(sources, ((0, 0), (0, 2 * radius), (0, 2 * radius)))
        returned = lax.optimization_barrier(jnp.sum(jnp.fft.fft2(sources, axes=(1, 2)) * adjoint_spectrum, axis=0))
        grad_data = 2.0 * jnp.real(jnp.fft.ifft2(returned))[:NX, :NY]
        padded = jnp.pad(extrapolated, ((0, 1), (0, 1)))
        step_down = padded[1:, :-1] - extrapolated
        step_side = padded[:-1, 1:] - extrapolated
        length = jnp.sqrt(step_down * step_down + step_side * step_side + EPS_TV)
        flow_down = step_down / length
        flow_side = step_side / length
        grad_tv = -(flow_down + flow_side)
        grad_tv = grad_tv + jnp.pad(flow_down, ((1, 0), (0, 0)))[:-1, :]
        grad_tv = grad_tv + jnp.pad(flow_side, ((0, 0), (1, 0)))[:, :-1]
        objective = jnp.sum((resist - target) ** 2) + TV_WEIGHT * jnp.sum(length) + L1_WEIGHT * jnp.sum(jnp.abs(extrapolated))
        totals.append(objective / (NX * NY))
        updated = jnp.clip(extrapolated - STEP_SIZE * (grad_data + TV_WEIGHT * grad_tv) - STEP_SIZE * L1_WEIGHT, 0.0, 1.0)
        previous = current
        current = updated
    return (current, previous, jnp.stack(totals))
```

```python
import functools
import math

import jax
import jax.numpy as jnp
import ml_dtypes
import numpy as np
from jax import lax
from jax.experimental import pallas as pl
from jax.experimental.pallas import tpu as pltpu
from jax.sharding import PartitionSpec as P

ITERS = 2
SLOPE = 4.0
LEVEL = 0.8
STEP_SIZE = 0.05
TV_WEIGHT = 0.05
L1_WEIGHT = 0.5
EPS_TV = 0.01
PRIOR_STEPS = 10.0

T = 128
N = 256
KS = 129
KP = 144
K = 8
R = 64
MESH = pl.DeviceIdType.MESH
F32 = jnp.float32
BF16 = jnp.bfloat16


def tables():
    pos = np.arange(N)
    shift = np.where(pos < T + R, pos, pos - N).astype(np.float64)
    tap = np.arange(N) - R
    alive = (np.arange(N) < KS).astype(np.float64)
    freq2 = np.arange(T) + 0.5
    freq1 = np.arange(N)
    step = 2.0 * math.pi / N

    def right(offset):
        phase = offset[:, None] * freq2[None, :] * step
        return np.concatenate([np.cos(phase), -np.sin(phase)], axis=1)

    def left(offset):
        phase = freq1[:, None] * offset[None, :] * step
        return np.concatenate([np.cos(phase), np.sin(phase)], axis=0)

    w = right(shift)
    wk = right(tap) * alive[:, None]
    d = left(pos)
    dk = left(tap) * alive[None, :]
    wi = w.T * (2.0 / (N * N))

    def half(odd):
        rows = 2 * np.arange(T // 2) + odd
        phase = rows[:, None] * np.arange(T)[None, :] * step
        c, s = np.cos(phase), np.sin(phase)
        return np.concatenate([np.concatenate([c, -s], 1), np.concatenate([s, c], 1)], 0)

    even, odd = half(0), half(1)
    both = np.concatenate([even.T, odd.T], axis=1)
    place, parts, row = {}, [], 0
    for name, table in (("w", w), ("wk", wk), ("d", d), ("dk", dk), ("even", even), ("odd", odd), ("both", both), ("wi", wi)):
        high = table.astype(np.float32).astype(ml_dtypes.bfloat16)
        low = (table - high.astype(np.float64)).astype(np.float32).astype(ml_dtypes.bfloat16)
        for which, part in (("h", high), ("l", low)):
            place[name + which] = (row, row + part.shape[0])
            parts.append(part)
            row += part.shape[0]
    return place, np.concatenate(parts, axis=0)


PLACE, TABLE = tables()


def split(x):
    high = x.astype(BF16)
    return high, (x - high.astype(F32)).astype(BF16)


def mm(a, b):
    return jnp.dot(a, b, preferred_element_type=F32)


def rows(*parts):
    return jnp.concatenate(parts, axis=0)


def lanes(*parts):
    return jnp.concatenate(parts, axis=1)


def kernel(
    size_r,
    size_c,
    mask_ref,
    prev_ref,
    target_ref,
    restart_ref,
    taps_hbm,
    table_hbm,
    next_ref,
    last_ref,
    goal_ref,
    taps_ref,
    table_ref,
    padded_ref,
    hr_ref,
    hi_ref,
    field_ref,
    gr_ref,
    gi_ref,
    point_ref,
    own_ref,
    ud_ref,
    lr_ref,
    corner_ref,
    goal_part,
    slots_ref,
    sums_ref,
    local_sem,
    send_sem,
    recv_sem,
    red_send,
    red_recv,
):
    r = lax.axis_index("row")
    c = lax.axis_index("col")
    near = []
    for dr, dc in ((1, 0), (-1, 0), (0, 1), (0, -1), (1, 1), (1, -1), (-1, 1), (-1, -1)):
        near.append((lax.rem(r + dr + size_r, size_r), lax.rem(c + dc + size_c, size_c)))
    low = min(8, size_r)
    high = size_r // low
    r_high, r_low = r // low, lax.rem(r, low)
    groups = []
    groups.append((c, [(r, lax.rem(c + d, size_c)) for d in range(1, size_c)]))
    groups.append((r_low, [(r_high * low + lax.rem(r_low + d, low), c) for d in range(1, low)]))
    groups.append((r_high, [(lax.rem(r_high + d, high) * low + r_low, c) for d in range(1, high)]))

    def tab(name):
        first, end = PLACE[name]
        return table_ref[first:end, :]

    taps_copy = pltpu.make_async_copy(taps_hbm, taps_ref, local_sem.at[0])
    table_copy = pltpu.make_async_copy(table_hbm, table_ref, local_sem.at[1])
    table_copy.start()
    taps_copy.start()
    barrier = pltpu.get_barrier_semaphore()
    everyone = near + [peer for _, peers in groups for peer in peers]
    for peer in everyone:
        pl.semaphore_signal(barrier, inc=1, device_id=peer, device_id_type=MESH)

    def extrapolate(t, current, previous):
        momentum = (t + PRIOR_STEPS - 1.0) / (t + PRIOR_STEPS + 2.0)
        keep = 1.0 - restart_ref[t, 0, 0].astype(F32)
        point_ref[t] = current + keep * momentum * (current - previous)

    def exchange(slot, down, up, side, corner_down, corner_up):
        copies = []
        pieces = (
            (down[0], ud_ref.at[slot, down[1]]),
            (up[0], ud_ref.at[slot, up[1]]),
            (side, lr_ref.at[slot, 0]),
            (side, lr_ref.at[slot, 1]),
            (corner_down, corner_ref.at[slot, 0, down[1]]),
            (corner_down, corner_ref.at[slot, 1, down[1]]),
            (corner_up, corner_ref.at[slot, 0, up[1]]),
            (corner_up, corner_ref.at[slot, 1, up[1]]),
        )
        for n, (source, target) in enumerate(pieces):
            copy = pltpu.make_async_remote_copy(
                src_ref=source,
                dst_ref=target,
                send_sem=send_sem.at[slot, n],
                recv_sem=recv_sem.at[slot, n],
                device_id=near[n],
                device_id_type=MESH,
            )
            copy.start()
            copies.append(copy)
        return copies

    top, bottom = pl.ds(0, R), pl.ds(R, R)

    def send_point(t):
        ref = point_ref.at[t]
        return exchange(2 * t, (ref.at[bottom], bottom), (ref.at[top], top), ref, ref.at[bottom], ref.at[top])

    def send_gradient(t):
        down, up = pl.ds(T, R), pl.ds(T + R, R)
        left_lanes, right_lanes = pl.ds(0, T), pl.ds(T, T)
        ref = own_ref.at[t]
        return exchange(
            2 * t + 1,
            (ref.at[down, left_lanes], top),
            (ref.at[up, left_lanes], bottom),
            ref.at[pl.ds(0, T), right_lanes],
            ref.at[down, right_lanes],
            ref.at[up, right_lanes],
        )

    def reduce_start(phase, value):
        me, peers = groups[phase]
        slots_ref[phase, me] = value
        sums_ref[phase] = value
        copies = []
        for d, peer in enumerate(peers):
            copy = pltpu.make_async_remote_copy(
                src_ref=sums_ref.at[phase],
                dst_ref=slots_ref.at[phase, me],
                send_sem=red_send.at[phase, d],
                recv_sem=red_recv.at[phase, d],
                device_id=peer,
                device_id_type=MESH,
            )
            copy.start()
            copies.append(copy)
        return copies

    def reduce_end(phase, copies):
        for copy in copies:
            copy.wait_recv()
        total = slots_ref[phase, 0]
        for n in range(1, len(copies) + 1):
            total = total + slots_ref[phase, n]
        return total

    row_id = lax.broadcasted_iota(jnp.int32, (T, T), 0)
    lane_id = lax.broadcasted_iota(jnp.int32, (T, T), 1)
    upper = row_id < R
    first_lanes = lane_id < R
    has_up, has_down = r > 0, r < size_r - 1
    has_left, has_right = c > 0, c < size_c - 1

    extrapolate(0, mask_ref[...], prev_ref[...])
    pl.semaphore_wait(barrier, len(everyone))
    sent = send_point(0)
    pending = list(sent)

    padded_ref[...] = jnp.zeros_like(padded_ref)
    taps_copy.wait()
    table_copy.wait()

    def spectrum(k, carry):
        for part in range(2):
            padded_ref[part, 0:KS, 0:KS] = taps_ref[k, part]
            xh, xl = split(padded_ref[part])
            y = mm(lanes(xh, xh, xl), rows(tab("wkh"), tab("wkl"), tab("wkh")))
            yh, yl = split(y)
            dh, dl = tab("dkh")[:, :KP], tab("dkl")[:, :KP]
            q = mm(dh, yh) + mm(dh, yl) + mm(dl, yh)
            hr_ref[k, :, part * T : (part + 1) * T] = q[:N, :T] + q[N:, T:]
            hi_ref[k, :, part * T : (part + 1) * T] = q[:N, T:] - q[N:, :T]
        return carry

    lax.fori_loop(0, K, spectrum, 0)

    previous = mask_ref[...]
    objective = []
    for t in range(ITERS):
        point = point_ref[t]
        slot = 2 * t
        for copy in sent:
            copy.wait_recv()
        zero = jnp.zeros((T, T), F32)
        rows_live = jnp.where(upper, has_down.astype(F32), has_up.astype(F32))
        lanes_live = jnp.where(first_lanes, has_right.astype(F32), has_left.astype(F32))
        below = ud_ref[slot] * rows_live
        beside = jnp.where(first_lanes, lr_ref[slot, 1], lr_ref[slot, 0]) * lanes_live
        corner = jnp.where(first_lanes, corner_ref[slot, 1], corner_ref[slot, 0]) * (rows_live * lanes_live)
        x = rows(lanes(point, beside), lanes(below, corner))

        strip = rows(x[N - 8 :], x[: T + 8])
        high_rows = strip.shape[0]
        step_down = pltpu.roll(strip, high_rows - 1, 0) - strip
        step_side = pltpu.roll(strip, N - 1, 1) - strip
        squared = step_down * step_down + step_side * step_side + EPS_TV
        inverse = lax.rsqrt(squared)
        flow_down = step_down * inverse
        flow_side = step_side * inverse
        from_up = pltpu.roll(flow_down, 1, 0)[8 : T + 8, :T]
        from_left = pltpu.roll(flow_side, 1, 1)[8 : T + 8, :T]
        from_up = jnp.where((row_id == 0) & (r == 0), zero, from_up)
        from_left = jnp.where((lane_id == 0) & (c == 0), zero, from_left)
        grad_tv = from_up + from_left - (flow_down + flow_side)[8 : T + 8, :T]
        length = (squared * inverse)[8 : T + 8, :T]

        xh, xl = split(x)
        a = mm(lanes(xh, xh, xl), rows(tab("wh"), tab("wl"), tab("wh")))
        ah, al = split(a)
        q = mm(lanes(tab("dh"), tab("dh"), tab("dl")), rows(ah, al, ah))
        mr = q[:N, :T] + q[N:, T:]
        mi = q[:N, T:] - q[N:, :T]
        gr_ref[...] = lanes(mr, mr)
        gi_ref[...] = lanes(mi, mi)

        def forward(k, total):
            m_r, m_i, h_r, h_i = gr_ref[...], gi_ref[...], hr_ref[k], hi_ref[k]
            p_r = m_r * h_r + m_i * h_i
            p_i = m_i * h_r - m_r * h_i
            plus = rows(p_r[:T] + p_r[T:], p_i[:T] + p_i[T:])
            minus = rows(p_r[:T] - p_r[T:], p_i[:T] - p_i[T:])
            bh, bl = split(plus)
            z_even = mm(lanes(tab("evenh"), tab("evenh"), tab("evenl")), rows(bh, bl, bh))
            bh, bl = split(minus)
            z_odd = mm(lanes(tab("oddh"), tab("oddh"), tab("oddl")), rows(bh, bl, bh))
            z = rows(
                lanes(z_even[:R, :T], z_even[R:, :T]),
                lanes(z_odd[:R, :T], z_odd[R:, :T]),
                lanes(z_even[:R, T:], z_even[R:, T:]),
                lanes(z_odd[:R, T:], z_odd[R:, T:]),
            )
            zh, zl = split(z)
            wi = lanes(tab("wih")[:, :T], tab("wil")[:, :T])
            e = mm(zh, wi)
            f = mm(zl, wi)
            e = (e[:, :T] + e[:, T:]) + (f[:, :T] + f[:, T:])
            field_ref[k] = e
            square = e * e
            return total + (square[:T] + square[T:])

        intensity = lax.fori_loop(0, K, forward, zero)
        wanted = rows(target_ref[pl.ds(0, R, stride=2), :], target_ref[pl.ds(1, R, stride=2), :])
        resist = 1.0 / (1.0 + jnp.exp(-SLOPE * (intensity - LEVEL)))
        miss = resist - wanted
        weight = 2.0 * miss * SLOPE * resist * (1.0 - resist)
        term = miss * miss + TV_WEIGHT * length + L1_WEIGHT * jnp.abs(point)
        goal_part[t] = jnp.sum(term.reshape(T // 8, 8, T), axis=0)

        gr_ref[...] = jnp.zeros_like(gr_ref)
        gi_ref[...] = jnp.zeros_like(gi_ref)
        weight2 = rows(weight, weight)

        def adjoint(k, carry):
            vh, vl = split(weight2 * field_ref[k])
            v = lanes(vh, vl)
            wh, wl = tab("wh")[:T], tab("wl")[:T]
            y = mm(v, rows(wh, wh)) + mm(v, rows(wl, wl))
            y_r = lanes(y[:T, :T], y[T:, :T])
            y_i = lanes(y[:T, T:], y[T:, T:])
            out = []
            for n in range(2):
                half = slice(n * R, (n + 1) * R)
                yh, yl = split(rows(y_r[half], y_i[half]))
                y2 = rows(yh, yl)
                bh = tab("bothh")[:, n * T : (n + 1) * T]
                bl = tab("bothl")[:, n * T : (n + 1) * T]
                out.append(mm(lanes(bh, bh), y2) + mm(lanes(bl, bl), y2))
            even, odd = out
            first = even + odd
            second = even - odd
            for n, s in enumerate((first, second)):
                at = slice(n * T, (n + 1) * T)
                s_r, s_i = s[:T], s[T:]
                h_r, h_i = hr_ref[k, at], hi_ref[k, at]
                gr_ref[at] += h_r * s_r - h_i * s_i
                gi_ref[at] += h_r * s_i + h_i * s_r
            return carry

        last = t == ITERS - 1
        reducing = None
        if last:
            line = lax.broadcasted_iota(jnp.int32, (8, T), 0)
            value = jnp.zeros((8, T), F32)
            for n in range(ITERS):
                value = jnp.where(line == n, jnp.sum(goal_part[n], axis=0, keepdims=True), value)
            reducing = reduce_start(0, value)
            pending += reducing
            lax.fori_loop(0, K // 2, adjoint, 0)
            reducing = reduce_start(1, reduce_end(0, reducing))
            pending += reducing
            lax.fori_loop(K // 2, K, adjoint, 0)
        else:
            lax.fori_loop(0, K, adjoint, 0)
        g = lanes(gr_ref[:, :T] + gr_ref[:, T:], gi_ref[:, :T] + gi_ref[:, T:])
        gh, gl = split(g)
        q = mm(lanes(tab("dh"), tab("dh"), tab("dl")), rows(gh, gl, gh))
        z = lanes(q[:N, :T] - q[N:, T:], q[:N, T:] + q[N:, :T])
        zh, zl = split(z)
        own_ref[t] = mm(lanes(zh, zh, zl), rows(tab("wih"), tab("wil"), tab("wih")))
        sent = send_gradient(t)
        pending += sent
        if last:
            reducing = reduce_start(2, reduce_end(1, reducing))
            pending += reducing
        for copy in sent:
            copy.wait_recv()
        slot = 2 * t + 1
        rows_live = jnp.where(upper, has_up.astype(F32), has_down.astype(F32))
        lanes_live = jnp.where(first_lanes, has_left.astype(F32), has_right.astype(F32))
        grad_data = own_ref[t, 0:T, 0:T] + ud_ref[slot] * rows_live
        beside = jnp.where(first_lanes, lr_ref[slot, 0], lr_ref[slot, 1])
        corner = jnp.where(first_lanes, corner_ref[slot, 0], corner_ref[slot, 1])
        grad_data = 2.0 * (grad_data + (beside + corner * rows_live) * lanes_live)
        updated = jnp.clip(
            point - STEP_SIZE * (grad_data + TV_WEIGHT * grad_tv) - STEP_SIZE * L1_WEIGHT, 0.0, 1.0
        )
        if last:
            next_ref[...] = updated
            total = reduce_end(2, reducing)
            scale = 1.0 / (size_r * size_c * T * T)
            for n in range(ITERS):
                goal_ref[n] = jnp.sum(total[n : n + 1]) * scale
        else:
            last_ref[...] = updated
            extrapolate(t + 1, updated, previous)
            previous = updated
            sent = send_point(t + 1)
            pending += sent
    for copy in pending:
        copy.wait_send()


def shards(size_r, size_c, mask, mask_prev, target, kernels, restart):
    vmem = pl.BlockSpec(memory_space=pltpu.VMEM)
    smem = pl.BlockSpec(memory_space=pltpu.SMEM)
    anywhere = pl.BlockSpec(memory_space=pl.ANY)
    low = min(8, size_r)
    widest = max(size_c, low, size_r // low)
    return pl.pallas_call(
        functools.partial(kernel, size_r, size_c),
        out_shape=(
            jax.ShapeDtypeStruct((T, T), F32),
            jax.ShapeDtypeStruct((T, T), F32),
            jax.ShapeDtypeStruct((ITERS,), F32),
        ),
        in_specs=[vmem, vmem, vmem, smem, anywhere, anywhere],
        out_specs=(vmem, vmem, smem),
        scratch_shapes=[
            pltpu.VMEM((K, 2, KS, KS), F32),
            pltpu.VMEM(TABLE.shape, BF16),
            pltpu.VMEM((2, KP, N), F32),
            pltpu.VMEM((K, N, N), F32),
            pltpu.VMEM((K, N, N), F32),
            pltpu.VMEM((K, N, T), F32),
            pltpu.VMEM((N, N), F32),
            pltpu.VMEM((N, N), F32),
            pltpu.VMEM((ITERS, T, T), F32),
            pltpu.VMEM((ITERS, N, N), F32),
            pltpu.VMEM((2 * ITERS, T, T), F32),
            pltpu.VMEM((2 * ITERS, 2, T, T), F32),
            pltpu.VMEM((2 * ITERS, 2, T, T), F32),
            pltpu.VMEM((ITERS, 8, T), F32),
            pltpu.VMEM((3, widest, 8, T), F32),
            pltpu.VMEM((3, 8, T), F32),
            pltpu.SemaphoreType.DMA((2,)),
            pltpu.SemaphoreType.DMA((2 * ITERS, 8)),
            pltpu.SemaphoreType.DMA((2 * ITERS, 8)),
            pltpu.SemaphoreType.DMA((3, widest)),
            pltpu.SemaphoreType.DMA((3, widest)),
        ],
        compiler_params=pltpu.CompilerParams(
            collective_id=0, has_side_effects=True, vmem_limit_bytes=48 * 1024 * 1024
        ),
        name="fista",
    )(mask, mask_prev, target, restart, kernels, jnp.asarray(TABLE))


def solution(mesh):
    in_specs = (P("row", "col"), P("row", "col"), P("row", "col"), P(), P(None, "row", "col"))
    out_specs = (P("row", "col"), P("row", "col"), P())
    body = functools.partial(shards, mesh.shape["row"], mesh.shape["col"])
    return jax.shard_map(body, mesh=mesh, in_specs=in_specs, out_specs=out_specs, check_vma=False)
```

```python
import functools
import math

import jax
import jax.numpy as jnp
import ml_dtypes
import numpy as np
from jax import lax
from jax.experimental import pallas as pl
from jax.experimental.pallas import tpu as pltpu
from jax.sharding import PartitionSpec as P

ITERS = 2
SLOPE = 4.0
LEVEL = 0.8
STEP_SIZE = 0.05
TV_WEIGHT = 0.05
L1_WEIGHT = 0.5
EPS_TV = 0.01
PRIOR_STEPS = 10.0

T = 128
N = 256
KS = 129
KP = 144
K = 8
R = 64
MESH = pl.DeviceIdType.MESH
F32 = jnp.float32
BF16 = jnp.bfloat16


def tables():
    pos = np.arange(N)
    shift = np.where(pos < T + R, pos, pos - N).astype(np.float64)
    tap = np.arange(N) - R
    alive = (np.arange(N) < KS).astype(np.float64)
    freq2 = np.arange(T) + 0.5
    freq1 = np.arange(N)
    step = 2.0 * math.pi / N

    def right(offset):
        phase = offset[:, None] * freq2[None, :] * step
        return np.concatenate([np.cos(phase), -np.sin(phase)], axis=1)

    def left(offset):
        phase = freq1[:, None] * offset[None, :] * step
        return np.concatenate([np.cos(phase), np.sin(phase)], axis=0)

    w = right(shift)
    wk = right(tap) * alive[:, None]
    d = left(pos)
    dk = left(tap) * alive[None, :]
    wi = w.T * (2.0 / (N * N))

    def half(odd):
        rows = 2 * np.arange(T // 2) + odd
        phase = rows[:, None] * np.arange(T)[None, :] * step
        c, s = np.cos(phase), np.sin(phase)
        return np.concatenate([np.concatenate([c, -s], 1), np.concatenate([s, c], 1)], 0)

    even, odd = half(0), half(1)
    both = np.concatenate([even.T, odd.T], axis=1)
    place, parts, row = {}, [], 0
    for name, table in (("w", w), ("wk", wk), ("d", d), ("dk", dk), ("even", even), ("odd", odd), ("both", both), ("wi", wi)):
        high = table.astype(np.float32).astype(ml_dtypes.bfloat16)
        low = (table - high.astype(np.float64)).astype(np.float32).astype(ml_dtypes.bfloat16)
        for which, part in (("h", high), ("l", low)):
            place[name + which] = (row, row + part.shape[0])
            parts.append(part)
            row += part.shape[0]
    return place, np.concatenate(parts, axis=0)


PLACE, TABLE = tables()


def split(x):
    high = x.astype(BF16)
    return high, (x - high.astype(F32)).astype(BF16)


def mm(a, b):
    return jnp.dot(a, b, preferred_element_type=F32)


def rows(*parts):
    return jnp.concatenate(parts, axis=0)


def lanes(*parts):
    return jnp.concatenate(parts, axis=1)


def kernel(
    size_r,
    size_c,
    mask_ref,
    prev_ref,
    target_ref,
    restart_ref,
    taps_hbm,
    table_hbm,
    next_ref,
    last_ref,
    goal_ref,
    taps_ref,
    table_ref,
    padded_ref,
    hr_ref,
    hi_ref,
    field_ref,
    gr_ref,
    gi_ref,
    point_ref,
    own_ref,
    ud_ref,
    side_ref,
    corner_ref,
    side_out,
    corner_out,
    goal_part,
    slots_ref,
    sums_ref,
    local_sem,
    send_sem,
    recv_sem,
    red_send,
    red_recv,
):
    r = lax.axis_index("row")
    c = lax.axis_index("col")
    near = {}
    for dr in (-1, 0, 1):
        for dc in (-1, 0, 1):
            if dr or dc:
                near[dr, dc] = (lax.rem(r + dr + size_r, size_r), lax.rem(c + dc + size_c, size_c))
    low = min(8, size_r)
    high = size_r // low
    r_high, r_low = r // low, lax.rem(r, low)
    groups = []
    groups.append((c, [(r, lax.rem(c + d, size_c)) for d in range(1, size_c)]))
    groups.append((r_low, [(r_high * low + lax.rem(r_low + d, low), c) for d in range(1, low)]))
    groups.append((r_high, [(lax.rem(r_high + d, high) * low + r_low, c) for d in range(1, high)]))

    def tab(name):
        first, end = PLACE[name]
        return table_ref[first:end, :]

    taps_copy = pltpu.make_async_copy(taps_hbm, taps_ref, local_sem.at[0])
    table_copy = pltpu.make_async_copy(table_hbm, table_ref, local_sem.at[1])
    table_copy.start()
    taps_copy.start()
    barrier = pltpu.get_barrier_semaphore()
    everyone = list(near.values()) + [peer for _, peers in groups for peer in peers]
    for peer in everyone:
        pl.semaphore_signal(barrier, inc=1, device_id=peer, device_id_type=MESH)

    def extrapolate(t, current, previous):
        momentum = (t + PRIOR_STEPS - 1.0) / (t + PRIOR_STEPS + 2.0)
        keep = 1.0 - restart_ref[0, 0, t].astype(F32)
        point = current + keep * momentum * (current - previous)
        point_ref[t] = point
        return point

    def exchange(slot, sign, beyond, beside, corner):
        side_out[slot, 0], side_out[slot, 1] = pack(beside)
        for h in range(2):
            corner_out[slot, h, 0], corner_out[slot, h, 1] = pack(corner[h * R : (h + 1) * R])
        pieces = []
        ways = (-sign, sign)
        for h in range(2):
            for p in range(2):
                pieces.append((ways[h], ways[p], corner_out.at[slot, h, p], corner_ref.at[slot, h, p]))
        for h in range(2):
            half = pl.ds(h * R, R)
            pieces.append((ways[h], 0, beyond.at[half], ud_ref.at[slot, half]))
        for p in range(2):
            pieces.append((0, ways[p], side_out.at[slot, p], side_ref.at[slot, p]))
        copies = []
        for n, (dr, dc, source, target) in enumerate(pieces):
            copy = pltpu.make_async_remote_copy(
                src_ref=source,
                dst_ref=target,
                send_sem=send_sem.at[slot, n],
                recv_sem=recv_sem.at[slot, n],
                device_id=near[dr, dc],
                device_id_type=MESH,
            )
            copy.start()
            copies.append(copy)
        return copies

    def pack(block):
        half = block.shape[0] // 2
        turned = pltpu.roll(block, R, 1)
        first = first_lanes[:half]
        return jnp.where(first, block[:half], turned[half:]), jnp.where(first, turned[:half], block[half:])

    def unpack(low, high):
        first = first_lanes[: low.shape[0]]
        return rows(jnp.where(first, low, pltpu.roll(high, R, 1)), jnp.where(first, pltpu.roll(low, R, 1), high))

    def arrived(slot):
        corner = rows(*(unpack(corner_ref[slot, h, 0], corner_ref[slot, h, 1]) for h in range(2)))
        return ud_ref[slot], unpack(side_ref[slot, 0], side_ref[slot, 1]), corner

    def send_point(t, point):
        return exchange(2 * t, 1, point_ref.at[t], point, point)

    def send_gradient(t, g):
        own_ref[t] = g[T:, :T]
        return exchange(2 * t + 1, -1, own_ref.at[t], g[:T, T:], g[T:, T:])

    def reduce_start(phase, value):
        me, peers = groups[phase]
        slots_ref[phase, me] = value
        sums_ref[phase] = value
        copies = []
        for d, peer in enumerate(peers):
            copy = pltpu.make_async_remote_copy(
                src_ref=sums_ref.at[phase],
                dst_ref=slots_ref.at[phase, me],
                send_sem=red_send.at[phase, d],
                recv_sem=red_recv.at[phase, d],
                device_id=peer,
                device_id_type=MESH,
            )
            copy.start()
            copies.append(copy)
        return copies

    def reduce_end(phase, copies):
        for copy in copies:
            copy.wait_recv()
        total = slots_ref[phase, 0]
        for n in range(1, len(copies) + 1):
            total = total + slots_ref[phase, n]
        return total

    row_id = lax.broadcasted_iota(jnp.int32, (T, T), 0)
    lane_id = lax.broadcasted_iota(jnp.int32, (T, T), 1)
    upper = row_id < R
    first_lanes = lane_id < R
    has_up, has_down = r > 0, r < size_r - 1
    has_left, has_right = c > 0, c < size_c - 1

    point = extrapolate(0, mask_ref[...], prev_ref[...])
    pl.semaphore_wait(barrier, len(everyone))
    sent = send_point(0, point)
    pending = list(sent)

    padded_ref[...] = jnp.zeros_like(padded_ref)
    taps_copy.wait()
    table_copy.wait()

    def spectrum(k, carry):
        for part in range(2):
            padded_ref[part, 0:KS, 0:KS] = taps_ref[k, part]
            xh, xl = split(padded_ref[part])
            y = mm(lanes(xh, xh, xl), rows(tab("wkh"), tab("wkl"), tab("wkh")))
            yh, yl = split(y)
            dh, dl = tab("dkh")[:, :KP], tab("dkl")[:, :KP]
            q = mm(dh, yh) + mm(dh, yl) + mm(dl, yh)
            hr_ref[k, :, part * T : (part + 1) * T] = q[:N, :T] + q[N:, T:]
            hi_ref[k, :, part * T : (part + 1) * T] = q[:N, T:] - q[N:, :T]
        return carry

    lax.fori_loop(0, K, spectrum, 0, unroll=True)

    previous = mask_ref[...]
    objective = []
    for t in range(ITERS):
        for copy in sent:
            copy.wait_recv()
        zero = jnp.zeros((T, T), F32)
        rows_live = jnp.where(upper, has_down.astype(F32), has_up.astype(F32))
        lanes_live = jnp.where(first_lanes, has_right.astype(F32), has_left.astype(F32))
        below, beside, corner = arrived(2 * t)
        below = below * rows_live
        beside = beside * lanes_live
        corner = corner * (rows_live * lanes_live)
        x = rows(lanes(point, beside), lanes(below, corner))

        strip = rows(x[N - 8 :], x[: T + 8])
        high_rows = strip.shape[0]
        step_down = pltpu.roll(strip, high_rows - 1, 0) - strip
        step_side = pltpu.roll(strip, N - 1, 1) - strip
        squared = step_down * step_down + step_side * step_side + EPS_TV
        inverse = lax.rsqrt(squared)
        flow_down = step_down * inverse
        flow_side = step_side * inverse
        from_up = pltpu.roll(flow_down, 1, 0)[8 : T + 8, :T]
        from_left = pltpu.roll(flow_side, 1, 1)[8 : T + 8, :T]
        from_up = jnp.where((row_id == 0) & (r == 0), zero, from_up)
        from_left = jnp.where((lane_id == 0) & (c == 0), zero, from_left)
        grad_tv = from_up + from_left - (flow_down + flow_side)[8 : T + 8, :T]
        length = (squared * inverse)[8 : T + 8, :T]

        xh, xl = split(x)
        a = mm(lanes(xh, xh, xl), rows(tab("wh"), tab("wl"), tab("wh")))
        ah, al = split(a)
        q = mm(lanes(tab("dh"), tab("dh"), tab("dl")), rows(ah, al, ah))
        mr = q[:N, :T] + q[N:, T:]
        mi = q[:N, T:] - q[N:, :T]
        gr_ref[...] = lanes(mr, mr)
        gi_ref[...] = lanes(mi, mi)

        def forward(k, total):
            m_r, m_i, h_r, h_i = gr_ref[...], gi_ref[...], hr_ref[k], hi_ref[k]
            p_r = m_r * h_r + m_i * h_i
            p_i = m_i * h_r - m_r * h_i
            plus = rows(p_r[:T] + p_r[T:], p_i[:T] + p_i[T:])
            minus = rows(p_r[:T] - p_r[T:], p_i[:T] - p_i[T:])
            bh, bl = split(plus)
            z_even = mm(lanes(tab("evenh"), tab("evenh"), tab("evenl")), rows(bh, bl, bh))
            bh, bl = split(minus)
            z_odd = mm(lanes(tab("oddh"), tab("oddh"), tab("oddl")), rows(bh, bl, bh))
            z = rows(
                lanes(z_even[:R, :T], z_even[R:, :T]),
                lanes(z_odd[:R, :T], z_odd[R:, :T]),
                lanes(z_even[:R, T:], z_even[R:, T:]),
                lanes(z_odd[:R, T:], z_odd[R:, T:]),
            )
            zh, zl = split(z)
            wi = lanes(tab("wih")[:, :T], tab("wil")[:, :T])
            e = mm(zh, wi)
            f = mm(zl, wi)
            e = (e[:, :T] + e[:, T:]) + (f[:, :T] + f[:, T:])
            field_ref[k] = e
            square = e * e
            return total + (square[:T] + square[T:])

        intensity = lax.fori_loop(0, K, forward, zero, unroll=True)
        wanted = rows(target_ref[pl.ds(0, R, stride=2), :], target_ref[pl.ds(1, R, stride=2), :])
        resist = 1.0 / (1.0 + jnp.exp(-SLOPE * (intensity - LEVEL)))
        miss = resist - wanted
        weight = 2.0 * miss * SLOPE * resist * (1.0 - resist)
        term = miss * miss + TV_WEIGHT * length + L1_WEIGHT * jnp.abs(point)
        goal_part[t] = jnp.sum(term.reshape(T // 8, 8, T), axis=0)

        gr_ref[...] = jnp.zeros_like(gr_ref)
        gi_ref[...] = jnp.zeros_like(gi_ref)
        weight2 = rows(weight, weight)

        def adjoint(k, carry):
            vh, vl = split(weight2 * field_ref[k])
            v = lanes(vh, vl)
            wh, wl = tab("wh")[:T], tab("wl")[:T]
            y = mm(v, rows(wh, wh)) + mm(v, rows(wl, wl))
            y_r = lanes(y[:T, :T], y[T:, :T])
            y_i = lanes(y[:T, T:], y[T:, T:])
            out = []
            for n in range(2):
                half = slice(n * R, (n + 1) * R)
                yh, yl = split(rows(y_r[half], y_i[half]))
                y2 = rows(yh, yl)
                bh = tab("bothh")[:, n * T : (n + 1) * T]
                bl = tab("bothl")[:, n * T : (n + 1) * T]
                out.append(mm(lanes(bh, bh), y2) + mm(lanes(bl, bl), y2))
            even, odd = out
            first = even + odd
            second = even - odd
            for n, s in enumerate((first, second)):
                at = slice(n * T, (n + 1) * T)
                s_r, s_i = s[:T], s[T:]
                h_r, h_i = hr_ref[k, at], hi_ref[k, at]
                gr_ref[at] += h_r * s_r - h_i * s_i
                gi_ref[at] += h_r * s_i + h_i * s_r
            return carry

        last = t == ITERS - 1
        reducing = None
        if last:
            line = lax.broadcasted_iota(jnp.int32, (8, T), 0)
            value = jnp.zeros((8, T), F32)
            for n in range(ITERS):
                value = jnp.where(line == n, jnp.sum(goal_part[n], axis=0, keepdims=True), value)
            reducing = reduce_start(0, value)
            pending += reducing
            lax.fori_loop(0, K // 2, adjoint, 0, unroll=True)
            reducing = reduce_start(1, reduce_end(0, reducing))
            pending += reducing
            lax.fori_loop(K // 2, K, adjoint, 0, unroll=True)
        else:
            lax.fori_loop(0, K, adjoint, 0, unroll=True)
        g = lanes(gr_ref[:, :T] + gr_ref[:, T:], gi_ref[:, :T] + gi_ref[:, T:])
        gh, gl = split(g)
        q = mm(lanes(tab("dh"), tab("dh"), tab("dl")), rows(gh, gl, gh))
        z = lanes(q[:N, :T] - q[N:, T:], q[:N, T:] + q[N:, :T])
        zh, zl = split(z)
        g = mm(lanes(zh, zh, zl), rows(tab("wih"), tab("wil"), tab("wih")))
        sent = send_gradient(t, g)
        pending += sent
        if last:
            reducing = reduce_start(2, reduce_end(1, reducing))
            pending += reducing
        for copy in sent:
            copy.wait_recv()
        rows_live = jnp.where(upper, has_up.astype(F32), has_down.astype(F32))
        lanes_live = jnp.where(first_lanes, has_left.astype(F32), has_right.astype(F32))
        below, beside, corner = arrived(2 * t + 1)
        grad_data = 2.0 * (g[:T, :T] + below * rows_live + (beside + corner * rows_live) * lanes_live)
        updated = jnp.clip(
            point - STEP_SIZE * (grad_data + TV_WEIGHT * grad_tv) - STEP_SIZE * L1_WEIGHT, 0.0, 1.0
        )
        if last:
            next_ref[...] = updated
            total = reduce_end(2, reducing)
            scale = 1.0 / (size_r * size_c * T * T)
            for n in range(ITERS):
                goal_ref[n] = jnp.sum(total[n : n + 1]) * scale
        else:
            last_ref[...] = updated
            point = extrapolate(t + 1, updated, previous)
            previous = updated
            sent = send_point(t + 1, point)
            pending += sent
    for copy in pending:
        copy.wait_send()


def shards(size_r, size_c, mask, mask_prev, target, kernels, restart):
    vmem = pl.BlockSpec(memory_space=pltpu.VMEM)
    smem = pl.BlockSpec(memory_space=pltpu.SMEM)
    anywhere = pl.BlockSpec(memory_space=pl.ANY)
    low = min(8, size_r)
    widest = max(size_c, low, size_r // low)
    return pl.pallas_call(
        functools.partial(kernel, size_r, size_c),
        out_shape=(
            jax.ShapeDtypeStruct((T, T), F32),
            jax.ShapeDtypeStruct((T, T), F32),
            jax.ShapeDtypeStruct((ITERS,), F32),
        ),
        in_specs=[vmem, vmem, vmem, smem, anywhere, anywhere],
        out_specs=(vmem, vmem, smem),
        scratch_shapes=[
            pltpu.VMEM((K, 2, KS, KS), F32),
            pltpu.VMEM(TABLE.shape, BF16),
            pltpu.VMEM((2, KP, N), F32),
            pltpu.VMEM((K, N, N), F32),
            pltpu.VMEM((K, N, N), F32),
            pltpu.VMEM((K, N, T), F32),
            pltpu.VMEM((N, N), F32),
            pltpu.VMEM((N, N), F32),
            pltpu.VMEM((ITERS, T, T), F32),
            pltpu.VMEM((ITERS, T, T), F32),
            pltpu.VMEM((2 * ITERS, T, T), F32),
            pltpu.VMEM((2 * ITERS, 2, R, T), F32),
            pltpu.VMEM((2 * ITERS, 2, 2, R // 2, T), F32),
            pltpu.VMEM((2 * ITERS, 2, R, T), F32),
            pltpu.VMEM((2 * ITERS, 2, 2, R // 2, T), F32),
            pltpu.VMEM((ITERS, 8, T), F32),
            pltpu.VMEM((3, widest, 8, T), F32),
            pltpu.VMEM((3, 8, T), F32),
            pltpu.SemaphoreType.DMA((2,)),
            pltpu.SemaphoreType.DMA((2 * ITERS, 8)),
            pltpu.SemaphoreType.DMA((2 * ITERS, 8)),
            pltpu.SemaphoreType.DMA((3, widest)),
            pltpu.SemaphoreType.DMA((3, widest)),
        ],
        compiler_params=pltpu.CompilerParams(
            collective_id=0, has_side_effects=True, vmem_limit_bytes=48 * 1024 * 1024
        ),
        name="fista",
    )(mask, mask_prev, target, jnp.transpose(restart, (1, 2, 0)), kernels, jnp.asarray(TABLE))


def solution(mesh):
    in_specs = (P("row", "col"), P("row", "col"), P("row", "col"), P(), P(None, "row", "col"))
    out_specs = (P("row", "col"), P("row", "col"), P())
    body = functools.partial(shards, mesh.shape["row"], mesh.shape["col"])
    return jax.shard_map(body, mesh=mesh, in_specs=in_specs, out_specs=out_specs, check_vma=False)
```

```python
import functools
import math

import jax
import jax.numpy as jnp
import ml_dtypes
import numpy as np
from jax import lax
from jax.experimental import pallas as pl
from jax.experimental.pallas import tpu as pltpu
from jax.sharding import PartitionSpec as P

ITERS = 2
SLOPE = 4.0
LEVEL = 0.8
STEP_SIZE = 0.05
TV_WEIGHT = 0.05
L1_WEIGHT = 0.5
EPS_TV = 0.01
PRIOR_STEPS = 10.0

T = 128
N = 256
KS = 129
KP = 144
K = 8
R = 64
MESH = pl.DeviceIdType.MESH
F32 = jnp.float32
BF16 = jnp.bfloat16


def tables():
    pos = np.arange(N)
    shift = np.where(pos < T + R, pos, pos - N).astype(np.float64)
    tap = np.arange(N) - R
    alive = (np.arange(N) < KS).astype(np.float64)
    freq2 = np.arange(T) + 0.5
    freq1 = np.arange(N)
    step = 2.0 * math.pi / N

    def right(offset):
        phase = offset[:, None] * freq2[None, :] * step
        return np.concatenate([np.cos(phase), -np.sin(phase)], axis=1)

    def left(offset):
        phase = freq1[:, None] * offset[None, :] * step
        return np.concatenate([np.cos(phase), np.sin(phase)], axis=0)

    w = right(shift)
    wk = right(tap) * alive[:, None]
    d = left(pos)
    dk = left(tap) * alive[None, :]
    wi = w.T * (2.0 / (N * N))

    def half(odd):
        rows = 2 * np.arange(T // 2) + odd
        phase = rows[:, None] * np.arange(T)[None, :] * step
        c, s = np.cos(phase), np.sin(phase)
        return np.concatenate([np.concatenate([c, -s], 1), np.concatenate([s, c], 1)], 0)

    even, odd = half(0), half(1)
    both = np.concatenate([even.T, odd.T], axis=1)
    place, parts, row = {}, [], 0
    for name, table in (("w", w), ("wk", wk), ("d", d), ("dk", dk), ("even", even), ("odd", odd), ("both", both), ("wi", wi)):
        high = table.astype(np.float32).astype(ml_dtypes.bfloat16)
        low = (table - high.astype(np.float64)).astype(np.float32).astype(ml_dtypes.bfloat16)
        for which, part in (("h", high), ("l", low)):
            place[name + which] = (row, row + part.shape[0])
            parts.append(part)
            row += part.shape[0]
    return place, np.concatenate(parts, axis=0)


PLACE, TABLE = tables()


def factors(size_r, size_c):
    core = math.gcd(size_r, 2)
    x = math.gcd(size_r // core, 4)
    y = math.gcd(size_c, 4)
    return (size_r // (core * x), x, core), (size_c // y, y)


def split(x):
    high = x.astype(BF16)
    return high, (x - high.astype(F32)).astype(BF16)


def mm(a, b):
    return jnp.dot(a, b, preferred_element_type=F32)


def rows(*parts):
    return jnp.concatenate(parts, axis=0)


def lanes(*parts):
    return jnp.concatenate(parts, axis=1)


def kernel(
    size_r,
    size_c,
    mask_ref,
    prev_ref,
    target_ref,
    restart_ref,
    taps_hbm,
    table_hbm,
    next_ref,
    last_ref,
    goal_ref,
    taps_ref,
    table_ref,
    padded_ref,
    hr_ref,
    hi_ref,
    field_ref,
    gr_ref,
    gi_ref,
    point_ref,
    own_ref,
    ud_ref,
    side_ref,
    corner_ref,
    side_out,
    corner_out,
    goal_part,
    slots_ref,
    sums_ref,
    local_sem,
    send_sem,
    recv_sem,
    red_send,
    red_recv,
):
    r = lax.axis_index("row")
    c = lax.axis_index("col")
    near = {}
    for dr in (-1, 0, 1):
        for dc in (-1, 0, 1):
            if dr or dc:
                near[dr, dc] = (lax.rem(r + dr + size_r, size_r), lax.rem(c + dc + size_c, size_c))
    rows_by, cols_by = factors(size_r, size_c)
    z_high, x, core = r // (rows_by[1] * rows_by[2]), lax.rem(r // rows_by[2], rows_by[1]), lax.rem(r, rows_by[2])
    z_low, y = c // cols_by[1], lax.rem(c, cols_by[1])

    def device(z_high, x, core, z_low, y):
        return (z_high * rows_by[1] + x) * rows_by[2] + core, z_low * cols_by[1] + y

    groups = []
    peers = []
    for i in range(rows_by[1]):
        for j in range(cols_by[1]):
            if i or j:
                peers.append(device(z_high, lax.rem(x + i, rows_by[1]), core, z_low, lax.rem(y + j, cols_by[1])))
    groups.append((x * cols_by[1] + y, peers))
    peers = []
    for i in range(rows_by[0]):
        for j in range(cols_by[0]):
            for k in range(rows_by[2]):
                if i or j or k:
                    peers.append(
                        device(
                            lax.rem(z_high + i, rows_by[0]), x, lax.rem(core + k, rows_by[2]), lax.rem(z_low + j, cols_by[0]), y
                        )
                    )
    groups.append(((z_high * cols_by[0] + z_low) * rows_by[2] + core, peers))

    def tab(name):
        first, end = PLACE[name]
        return table_ref[first:end, :]

    taps_copy = pltpu.make_async_copy(taps_hbm, taps_ref, local_sem.at[0])
    table_copy = pltpu.make_async_copy(table_hbm, table_ref, local_sem.at[1])
    table_copy.start()
    taps_copy.start()
    barrier = pltpu.get_barrier_semaphore()
    everyone = list(near.values()) + [peer for _, peers in groups for peer in peers]
    for peer in everyone:
        pl.semaphore_signal(barrier, inc=1, device_id=peer, device_id_type=MESH)

    def extrapolate(t, current, previous):
        momentum = (t + PRIOR_STEPS - 1.0) / (t + PRIOR_STEPS + 2.0)
        keep = 1.0 - restart_ref[0, 0, t].astype(F32)
        point = current + keep * momentum * (current - previous)
        point_ref[t] = point
        return point

    def exchange(slot, sign, beyond, beside, corner):
        side_out[slot, 0], side_out[slot, 1] = pack(beside)
        for h in range(2):
            corner_out[slot, h, 0], corner_out[slot, h, 1] = pack(corner[h * R : (h + 1) * R])
        pieces = []
        ways = (-sign, sign)
        for h in range(2):
            for p in range(2):
                pieces.append((ways[h], ways[p], corner_out.at[slot, h, p], corner_ref.at[slot, h, p]))
        for h in range(2):
            half = pl.ds(h * R, R)
            pieces.append((ways[h], 0, beyond.at[half], ud_ref.at[slot, half]))
        for p in range(2):
            pieces.append((0, ways[p], side_out.at[slot, p], side_ref.at[slot, p]))
        copies = []
        for n, (dr, dc, source, target) in enumerate(pieces):
            copy = pltpu.make_async_remote_copy(
                src_ref=source,
                dst_ref=target,
                send_sem=send_sem.at[slot, n],
                recv_sem=recv_sem.at[slot, n],
                device_id=near[dr, dc],
                device_id_type=MESH,
            )
            copy.start()
            copies.append(copy)
        return copies

    def pack(block):
        half = block.shape[0] // 2
        turned = pltpu.roll(block, R, 1)
        first = first_lanes[:half]
        return jnp.where(first, block[:half], turned[half:]), jnp.where(first, turned[:half], block[half:])

    def unpack(low, high):
        first = first_lanes[: low.shape[0]]
        return rows(jnp.where(first, low, pltpu.roll(high, R, 1)), jnp.where(first, pltpu.roll(low, R, 1), high))

    def arrived(slot):
        corner = rows(*(unpack(corner_ref[slot, h, 0], corner_ref[slot, h, 1]) for h in range(2)))
        return ud_ref[slot], unpack(side_ref[slot, 0], side_ref[slot, 1]), corner

    def send_point(t, point):
        return exchange(2 * t, 1, point_ref.at[t], point, point)

    def send_gradient(t, g):
        own_ref[t] = g[T:, :T]
        return exchange(2 * t + 1, -1, own_ref.at[t], g[:T, T:], g[T:, T:])

    def reduce_start(phase, value):
        me, peers = groups[phase]
        slots_ref[phase, me] = value
        sums_ref[phase] = value
        copies = []
        for d, peer in enumerate(peers):
            copy = pltpu.make_async_remote_copy(
                src_ref=sums_ref.at[phase],
                dst_ref=slots_ref.at[phase, me],
                send_sem=red_send.at[phase, d],
                recv_sem=red_recv.at[phase, d],
                device_id=peer,
                device_id_type=MESH,
            )
            copy.start()
            copies.append(copy)
        return copies

    def reduce_end(phase, copies):
        for copy in copies:
            copy.wait_recv()
        total = slots_ref[phase, 0]
        for n in range(1, len(copies) + 1):
            total = total + slots_ref[phase, n]
        return total

    row_id = lax.broadcasted_iota(jnp.int32, (T, T), 0)
    lane_id = lax.broadcasted_iota(jnp.int32, (T, T), 1)
    upper = row_id < R
    first_lanes = lane_id < R
    has_up, has_down = r > 0, r < size_r - 1
    has_left, has_right = c > 0, c < size_c - 1

    point = extrapolate(0, mask_ref[...], prev_ref[...])
    pl.semaphore_wait(barrier, len(everyone))
    sent = send_point(0, point)
    pending = list(sent)

    padded_ref[...] = jnp.zeros_like(padded_ref)
    taps_copy.wait()
    table_copy.wait()

    def spectrum(k, carry):
        for part in range(2):
            padded_ref[part, 0:KS, 0:KS] = taps_ref[k, :, part, :]
            xh, xl = split(padded_ref[part])
            y = mm(lanes(xh, xh, xl), rows(tab("wkh"), tab("wkl"), tab("wkh")))
            yh, yl = split(y)
            dh, dl = tab("dkh")[:, :KP], tab("dkl")[:, :KP]
            q = mm(dh, yh) + mm(dh, yl) + mm(dl, yh)
            hr_ref[k, :, part * T : (part + 1) * T] = q[:N, :T] + q[N:, T:]
            hi_ref[k, :, part * T : (part + 1) * T] = q[:N, T:] - q[N:, :T]
        return carry

    lax.fori_loop(0, K, spectrum, 0, unroll=True)

    previous = mask_ref[...]
    objective = []
    for t in range(ITERS):
        for copy in sent:
            copy.wait_recv()
        zero = jnp.zeros((T, T), F32)
        rows_live = jnp.where(upper, has_down.astype(F32), has_up.astype(F32))
        lanes_live = jnp.where(first_lanes, has_right.astype(F32), has_left.astype(F32))
        below, beside, corner = arrived(2 * t)
        below = below * rows_live
        beside = beside * lanes_live
        corner = corner * (rows_live * lanes_live)
        x = rows(lanes(point, beside), lanes(below, corner))

        strip = rows(x[N - 8 :], x[: T + 8])
        high_rows = strip.shape[0]
        step_down = pltpu.roll(strip, high_rows - 1, 0) - strip
        step_side = pltpu.roll(strip, N - 1, 1) - strip
        squared = step_down * step_down + step_side * step_side + EPS_TV
        inverse = lax.rsqrt(squared)
        flow_down = step_down * inverse
        flow_side = step_side * inverse
        from_up = pltpu.roll(flow_down, 1, 0)[8 : T + 8, :T]
        from_left = pltpu.roll(flow_side, 1, 1)[8 : T + 8, :T]
        from_up = jnp.where((row_id == 0) & (r == 0), zero, from_up)
        from_left = jnp.where((lane_id == 0) & (c == 0), zero, from_left)
        grad_tv = from_up + from_left - (flow_down + flow_side)[8 : T + 8, :T]
        length = (squared * inverse)[8 : T + 8, :T]

        xh, xl = split(x)
        a = mm(lanes(xh, xh, xl), rows(tab("wh"), tab("wl"), tab("wh")))
        ah, al = split(a)
        q = mm(lanes(tab("dh"), tab("dh"), tab("dl")), rows(ah, al, ah))
        mr = q[:N, :T] + q[N:, T:]
        mi = q[:N, T:] - q[N:, :T]
        gr_ref[...] = lanes(mr, mr)
        gi_ref[...] = lanes(mi, mi)

        def forward(k, total):
            m_r, m_i, h_r, h_i = gr_ref[...], gi_ref[...], hr_ref[k], hi_ref[k]
            p_r = m_r * h_r + m_i * h_i
            p_i = m_i * h_r - m_r * h_i
            plus = rows(p_r[:T] + p_r[T:], p_i[:T] + p_i[T:])
            minus = rows(p_r[:T] - p_r[T:], p_i[:T] - p_i[T:])
            bh, bl = split(plus)
            z_even = mm(lanes(tab("evenh"), tab("evenh"), tab("evenl")), rows(bh, bl, bh))
            bh, bl = split(minus)
            z_odd = mm(lanes(tab("oddh"), tab("oddh"), tab("oddl")), rows(bh, bl, bh))
            z = rows(
                lanes(z_even[:R, :T], z_even[R:, :T]),
                lanes(z_odd[:R, :T], z_odd[R:, :T]),
                lanes(z_even[:R, T:], z_even[R:, T:]),
                lanes(z_odd[:R, T:], z_odd[R:, T:]),
            )
            zh, zl = split(z)
            wi = lanes(tab("wih")[:, :T], tab("wil")[:, :T])
            e = mm(zh, wi)
            f = mm(zl, wi)
            e = (e[:, :T] + e[:, T:]) + (f[:, :T] + f[:, T:])
            field_ref[k] = e
            square = e * e
            return total + (square[:T] + square[T:])

        intensity = lax.fori_loop(0, K, forward, zero, unroll=True)
        wanted = rows(target_ref[pl.ds(0, R, stride=2), :], target_ref[pl.ds(1, R, stride=2), :])
        resist = 1.0 / (1.0 + jnp.exp(-SLOPE * (intensity - LEVEL)))
        miss = resist - wanted
        weight = 2.0 * miss * SLOPE * resist * (1.0 - resist)
        term = miss * miss + TV_WEIGHT * length + L1_WEIGHT * jnp.abs(point)
        goal_part[t] = jnp.sum(term.reshape(T // 8, 8, T), axis=0)

        gr_ref[...] = jnp.zeros_like(gr_ref)
        gi_ref[...] = jnp.zeros_like(gi_ref)
        weight2 = rows(weight, weight)

        def adjoint(k, carry):
            vh, vl = split(weight2 * field_ref[k])
            v = lanes(vh, vl)
            wh, wl = tab("wh")[:T], tab("wl")[:T]
            y = mm(v, rows(wh, wh)) + mm(v, rows(wl, wl))
            y_r = lanes(y[:T, :T], y[T:, :T])
            y_i = lanes(y[:T, T:], y[T:, T:])
            out = []
            for n in range(2):
                half = slice(n * R, (n + 1) * R)
                yh, yl = split(rows(y_r[half], y_i[half]))
                y2 = rows(yh, yl)
                bh = tab("bothh")[:, n * T : (n + 1) * T]
                bl = tab("bothl")[:, n * T : (n + 1) * T]
                out.append(mm(lanes(bh, bh), y2) + mm(lanes(bl, bl), y2))
            even, odd = out
            first = even + odd
            second = even - odd
            for n, s in enumerate((first, second)):
                at = slice(n * T, (n + 1) * T)
                s_r, s_i = s[:T], s[T:]
                h_r, h_i = hr_ref[k, at], hi_ref[k, at]
                gr_ref[at] += h_r * s_r - h_i * s_i
                gi_ref[at] += h_r * s_i + h_i * s_r
            return carry

        last = t == ITERS - 1
        reducing = None
        if last:
            line = lax.broadcasted_iota(jnp.int32, (8, T), 0)
            value = jnp.zeros((8, T), F32)
            for n in range(ITERS):
                value = jnp.where(line == n, jnp.sum(goal_part[n], axis=0, keepdims=True), value)
            reducing = reduce_start(0, value)
            pending += reducing
        lax.fori_loop(0, K, adjoint, 0, unroll=True)
        g = lanes(gr_ref[:, :T] + gr_ref[:, T:], gi_ref[:, :T] + gi_ref[:, T:])
        gh, gl = split(g)
        q = mm(lanes(tab("dh"), tab("dh"), tab("dl")), rows(gh, gl, gh))
        z = lanes(q[:N, :T] - q[N:, T:], q[:N, T:] + q[N:, :T])
        zh, zl = split(z)
        g = mm(lanes(zh, zh, zl), rows(tab("wih"), tab("wil"), tab("wih")))
        sent = send_gradient(t, g)
        pending += sent
        if last:
            reducing = reduce_start(1, reduce_end(0, reducing))
            pending += reducing
        for copy in sent:
            copy.wait_recv()
        rows_live = jnp.where(upper, has_up.astype(F32), has_down.astype(F32))
        lanes_live = jnp.where(first_lanes, has_left.astype(F32), has_right.astype(F32))
        below, beside, corner = arrived(2 * t + 1)
        grad_data = 2.0 * (g[:T, :T] + below * rows_live + (beside + corner * rows_live) * lanes_live)
        updated = jnp.clip(
            point - STEP_SIZE * (grad_data + TV_WEIGHT * grad_tv) - STEP_SIZE * L1_WEIGHT, 0.0, 1.0
        )
        if last:
            next_ref[...] = updated
            total = reduce_end(1, reducing)
            scale = 1.0 / (size_r * size_c * T * T)
            for n in range(ITERS):
                goal_ref[n] = jnp.sum(total[n : n + 1]) * scale
        else:
            last_ref[...] = updated
            point = extrapolate(t + 1, updated, previous)
            previous = updated
            sent = send_point(t + 1, point)
            pending += sent
    for copy in pending:
        copy.wait_send()


def shards(size_r, size_c, mask, mask_prev, target, kernels, restart):
    vmem = pl.BlockSpec(memory_space=pltpu.VMEM)
    smem = pl.BlockSpec(memory_space=pltpu.SMEM)
    anywhere = pl.BlockSpec(memory_space=pltpu.HBM)
    rows_by, cols_by = factors(size_r, size_c)
    widest = max(rows_by[1] * cols_by[1], rows_by[0] * cols_by[0] * rows_by[2])
    results = pl.pallas_call(
        functools.partial(kernel, size_r, size_c),
        out_shape=(
            jax.ShapeDtypeStruct((T, T), F32),
            jax.ShapeDtypeStruct((T, T), F32),
            jax.ShapeDtypeStruct((ITERS,), F32),
        ),
        in_specs=[vmem, vmem, vmem, smem, anywhere, anywhere],
        out_specs=(vmem, vmem, smem),
        scratch_shapes=[
            pltpu.VMEM((K, KS, 2, KS), F32),
            pltpu.VMEM(TABLE.shape, BF16),
            pltpu.VMEM((2, KP, N), F32),
            pltpu.VMEM((K, N, N), F32),
            pltpu.VMEM((K, N, N), F32),
            pltpu.VMEM((K, N, T), F32),
            pltpu.VMEM((N, N), F32),
            pltpu.VMEM((N, N), F32),
            pltpu.VMEM((ITERS, T, T), F32),
            pltpu.VMEM((ITERS, T, T), F32),
            pltpu.VMEM((2 * ITERS, T, T), F32),
            pltpu.VMEM((2 * ITERS, 2, R, T), F32),
            pltpu.VMEM((2 * ITERS, 2, 2, R // 2, T), F32),
            pltpu.VMEM((2 * ITERS, 2, R, T), F32),
            pltpu.VMEM((2 * ITERS, 2, 2, R // 2, T), F32),
            pltpu.VMEM((ITERS, 8, T), F32),
            pltpu.VMEM((2, widest, 8, T), F32),
            pltpu.VMEM((2, 8, T), F32),
            pltpu.SemaphoreType.DMA((2,)),
            pltpu.SemaphoreType.DMA((2 * ITERS, 8)),
            pltpu.SemaphoreType.DMA((2 * ITERS, 8)),
            pltpu.SemaphoreType.DMA((2, widest)),
            pltpu.SemaphoreType.DMA((2, widest)),
        ],
        compiler_params=pltpu.CompilerParams(
            collective_id=0, has_side_effects=True, vmem_limit_bytes=62 * 1024 * 1024
        ),
        name="fista",
    )(mask, mask_prev, target, jnp.transpose(restart, (1, 2, 0)), jnp.transpose(kernels, (0, 2, 1, 3)), jnp.asarray(TABLE))
    return pl.pallas_call(
        store,
        out_shape=tuple(jax.ShapeDtypeStruct(x.shape, x.dtype) for x in results),
        in_specs=[vmem, vmem, vmem],
        out_specs=(anywhere, anywhere, anywhere),
        scratch_shapes=[pltpu.SemaphoreType.DMA((3,))],
        name="store",
    )(*results)


def store(a_ref, b_ref, c_ref, next_ref, last_ref, goal_ref, sems):
    pairs = ((a_ref, next_ref), (b_ref, last_ref), (c_ref, goal_ref))
    copies = [pltpu.make_async_copy(x, y, sems.at[n]) for n, (x, y) in enumerate(pairs)]
    for copy in copies:
        copy.start()
    for copy in copies:
        copy.wait()


def solution(mesh):
    in_specs = (P("row", "col"), P("row", "col"), P("row", "col"), P(), P(None, "row", "col"))
    out_specs = (P("row", "col"), P("row", "col"), P())
    body = functools.partial(shards, mesh.shape["row"], mesh.shape["col"])
    return jax.shard_map(body, mesh=mesh, in_specs=in_specs, out_specs=out_specs, check_vma=False)
```

```python
import functools
import math

import jax
import jax.numpy as jnp
import ml_dtypes
import numpy as np
from jax import lax
from jax.experimental import pallas as pl
from jax.experimental.pallas import tpu as pltpu
from jax.sharding import PartitionSpec as P

ITERS = 2
SLOPE = 4.0
LEVEL = 0.8
STEP_SIZE = 0.05
TV_WEIGHT = 0.05
L1_WEIGHT = 0.5
EPS_TV = 0.01
PRIOR_STEPS = 10.0

T = 128
N = 256
KS = 129
KP = 144
K = 8
R = 64
CH = 16
MESH = pl.DeviceIdType.MESH
F32 = jnp.float32
BF16 = jnp.bfloat16


def tables():
    pos = np.arange(N)
    shift = np.where(pos < T + R, pos, pos - N).astype(np.float64)
    tap = np.arange(N) - R
    alive = (np.arange(N) < KS).astype(np.float64)
    freq2 = np.arange(T) + 0.5
    freq1 = np.arange(N)
    step = 2.0 * math.pi / N

    def right(offset):
        phase = offset[:, None] * freq2[None, :] * step
        return np.concatenate([np.cos(phase), -np.sin(phase)], axis=1)

    def left(offset):
        phase = freq1[:, None] * offset[None, :] * step
        return np.concatenate([np.cos(phase), np.sin(phase)], axis=0)

    w = right(shift)
    wk = right(tap) * alive[:, None]
    d = left(pos)
    dk = left(tap) * alive[None, :]
    wi = w.T * (2.0 / (N * N))

    def half(odd):
        rows = 2 * np.arange(T // 2) + odd
        phase = rows[:, None] * np.arange(T)[None, :] * step
        c, s = np.cos(phase), np.sin(phase)
        return np.concatenate([np.concatenate([c, -s], 1), np.concatenate([s, c], 1)], 0)

    even, odd = half(0), half(1)
    both = np.concatenate([even.T, odd.T], axis=1)
    place, parts, row = {}, [], 0
    for name, table in (("w", w), ("wk", wk), ("d", d), ("dk", dk), ("even", even), ("odd", odd), ("both", both), ("wi", wi)):
        high = table.astype(np.float32).astype(ml_dtypes.bfloat16)
        low = (table - high.astype(np.float64)).astype(np.float32).astype(ml_dtypes.bfloat16)
        for which, part in (("h", high), ("l", low)):
            place[name + which] = (row, row + part.shape[0])
            parts.append(part)
            row += part.shape[0]
    return place, np.concatenate(parts, axis=0)


PLACE, TABLE = tables()


def factors(size_r, size_c):
    core = math.gcd(size_r, 2)
    x = math.gcd(size_r // core, 4)
    y = math.gcd(size_c, 4)
    return (size_r // (core * x), x, core), (size_c // y, y)


def split(x):
    high = x.astype(BF16)
    return high, (x - high.astype(F32)).astype(BF16)


def mm(a, b):
    return jnp.dot(a, b, preferred_element_type=F32)


def rows(*parts):
    return jnp.concatenate(parts, axis=0)


def lanes(*parts):
    return jnp.concatenate(parts, axis=1)


def kernel(
    size_r,
    size_c,
    mask_hbm,
    prev_hbm,
    target_hbm,
    restart_hbm,
    taps_hbm,
    table_hbm,
    next_hbm,
    last_hbm,
    goal_ref,
    next_ref,
    last_ref,
    mask_ref,
    prev_ref,
    target_ref,
    restart_ref,
    taps_ref,
    table_ref,
    padded_ref,
    hr_ref,
    hi_ref,
    field_ref,
    gr_ref,
    gi_ref,
    point_ref,
    own_ref,
    b_ref,
    z_ref,
    v_ref,
    y_ref,
    m_ref,
    ud_ref,
    side_ref,
    corner_ref,
    side_out,
    corner_out,
    goal_part,
    slots_ref,
    sums_ref,
    local_sem,
    send_sem,
    recv_sem,
    red_send,
    red_recv,
):
    r = lax.axis_index("row")
    c = lax.axis_index("col")
    near = {}
    for dr in (-1, 0, 1):
        for dc in (-1, 0, 1):
            if dr or dc:
                near[dr, dc] = (lax.rem(r + dr + size_r, size_r), lax.rem(c + dc + size_c, size_c))
    rows_by, cols_by = factors(size_r, size_c)
    z_high, x, core = r // (rows_by[1] * rows_by[2]), lax.rem(r // rows_by[2], rows_by[1]), lax.rem(r, rows_by[2])
    z_low, y = c // cols_by[1], lax.rem(c, cols_by[1])

    def device(z_high, x, core, z_low, y):
        return (z_high * rows_by[1] + x) * rows_by[2] + core, z_low * cols_by[1] + y

    groups = []
    peers = []
    for i in range(rows_by[1]):
        for j in range(cols_by[1]):
            if i or j:
                peers.append(device(z_high, lax.rem(x + i, rows_by[1]), core, z_low, lax.rem(y + j, cols_by[1])))
    groups.append((x * cols_by[1] + y, peers))
    peers = []
    for i in range(rows_by[0]):
        for j in range(cols_by[0]):
            for k in range(rows_by[2]):
                if i or j or k:
                    peers.append(
                        device(
                            lax.rem(z_high + i, rows_by[0]), x, lax.rem(core + k, rows_by[2]), lax.rem(z_low + j, cols_by[0]), y
                        )
                    )
    groups.append(((z_high * cols_by[0] + z_low) * rows_by[2] + core, peers))

    def tab(name):
        first, end = PLACE[name]
        return table_ref[first:end, :]

    loads = []
    for n, (source, target) in enumerate(
        (
            (mask_hbm, mask_ref),
            (prev_hbm, prev_ref),
            (restart_hbm, restart_ref),
            (table_hbm, table_ref),
            (taps_hbm, taps_ref),
            (target_hbm, target_ref),
        )
    ):
        copy = pltpu.make_async_copy(source, target, local_sem.at[n])
        loads.append(copy)
    for copy in loads[:3]:
        copy.start()
    barrier = pltpu.get_barrier_semaphore()
    everyone = list(near.values()) + [peer for _, peers in groups for peer in peers]
    for peer in everyone:
        pl.semaphore_signal(barrier, inc=1, device_id=peer, device_id_type=MESH)
    for copy in loads[3:]:
        copy.start()

    stored = []

    def put(n, source, target):
        copy = pltpu.make_async_copy(source, target, local_sem.at[6 + n])
        copy.start()
        stored.append(copy)

    def extrapolate(t, current, previous):
        momentum = (t + PRIOR_STEPS - 1.0) / (t + PRIOR_STEPS + 2.0)
        keep = 1.0 - restart_ref[0, 0, t].astype(F32)
        point = current + keep * momentum * (current - previous)
        point_ref[t] = point
        return point

    def exchange(slot, sign, beyond, beside, corner):
        side_out[slot, 0], side_out[slot, 1] = pack(beside)
        for h in range(2):
            corner_out[slot, h, 0], corner_out[slot, h, 1] = pack(corner[h * R : (h + 1) * R])
        pieces = []
        ways = (-sign, sign)
        for h in range(2):
            for p in range(2):
                pieces.append((ways[h], ways[p], corner_out.at[slot, h, p], corner_ref.at[slot, h, p]))
        for h in range(2):
            half = pl.ds(h * R, R)
            pieces.append((ways[h], 0, beyond.at[half], ud_ref.at[slot, half]))
        for p in range(2):
            pieces.append((0, ways[p], side_out.at[slot, p], side_ref.at[slot, p]))
        copies = []
        for n, (dr, dc, source, target) in enumerate(pieces):
            copy = pltpu.make_async_remote_copy(
                src_ref=source,
                dst_ref=target,
                send_sem=send_sem.at[slot, n],
                recv_sem=recv_sem.at[slot, n],
                device_id=near[dr, dc],
                device_id_type=MESH,
            )
            copy.start()
            copies.append(copy)
        return copies

    def pack(block):
        half = block.shape[0] // 2
        turned = pltpu.roll(block, R, 1)
        first = first_lanes[:half]
        return jnp.where(first, block[:half], turned[half:]), jnp.where(first, turned[:half], block[half:])

    def unpack(low, high):
        first = first_lanes[: low.shape[0]]
        return rows(jnp.where(first, low, pltpu.roll(high, R, 1)), jnp.where(first, pltpu.roll(low, R, 1), high))

    def arrived(slot):
        corner = rows(*(unpack(corner_ref[slot, h, 0], corner_ref[slot, h, 1]) for h in range(2)))
        return ud_ref[slot], unpack(side_ref[slot, 0], side_ref[slot, 1]), corner

    def send_point(t, point):
        return exchange(2 * t, 1, point_ref.at[t], point, point)

    def send_gradient(t, g):
        own_ref[t] = g[T:, :T]
        return exchange(2 * t + 1, -1, own_ref.at[t], g[:T, T:], g[T:, T:])

    def reduce_start(phase, value):
        me, peers = groups[phase]
        slots_ref[phase, me] = value
        sums_ref[phase] = value
        copies = []
        for d, peer in enumerate(peers):
            copy = pltpu.make_async_remote_copy(
                src_ref=sums_ref.at[phase],
                dst_ref=slots_ref.at[phase, me],
                send_sem=red_send.at[phase, d],
                recv_sem=red_recv.at[phase, d],
                device_id=peer,
                device_id_type=MESH,
            )
            copy.start()
            copies.append(copy)
        return copies

    def reduce_end(phase, copies):
        for copy in copies:
            copy.wait_recv()
        total = slots_ref[phase, 0]
        for n in range(1, len(copies) + 1):
            total = total + slots_ref[phase, n]
        return total

    row_id = lax.broadcasted_iota(jnp.int32, (T, T), 0)
    lane_id = lax.broadcasted_iota(jnp.int32, (T, T), 1)
    upper = row_id < R
    first_lanes = lane_id < R
    has_up, has_down = r > 0, r < size_r - 1
    has_left, has_right = c > 0, c < size_c - 1

    for copy in loads[:3]:
        copy.wait()
    point = extrapolate(0, mask_ref[...], prev_ref[...])
    pl.semaphore_wait(barrier, len(everyone))
    sent = send_point(0, point)
    pending = list(sent)

    padded_ref[...] = jnp.zeros_like(padded_ref)
    for copy in loads[3:]:
        copy.wait()

    def spectrum(k, carry):
        for part in range(2):
            padded_ref[part, 0:KS, 0:KS] = taps_ref[k, :, part, :]
            xh, xl = split(padded_ref[part])
            y = mm(lanes(xh, xh, xl), rows(tab("wkh"), tab("wkl"), tab("wkh")))
            yh, yl = split(y)
            dh, dl = tab("dkh")[:, :KP], tab("dkl")[:, :KP]
            q = mm(dh, yh) + mm(dh, yl) + mm(dl, yh)
            hr_ref[k, :, part * T : (part + 1) * T] = q[:N, :T] + q[N:, T:]
            hi_ref[k, :, part * T : (part + 1) * T] = q[:N, T:] - q[N:, :T]
        return carry

    lax.fori_loop(0, K, spectrum, 0, unroll=True)

    previous = mask_ref[...]
    objective = []
    for t in range(ITERS):
        for copy in sent:
            copy.wait_recv()
        zero = jnp.zeros((T, T), F32)
        rows_live = jnp.where(upper, has_down.astype(F32), has_up.astype(F32))
        lanes_live = jnp.where(first_lanes, has_right.astype(F32), has_left.astype(F32))
        below, beside, corner = arrived(2 * t)
        below = below * rows_live
        beside = beside * lanes_live
        corner = corner * (rows_live * lanes_live)
        x = rows(lanes(point, beside), lanes(below, corner))

        strip = rows(x[N - 8 :], x[: T + 8])
        high_rows = strip.shape[0]
        step_down = pltpu.roll(strip, high_rows - 1, 0) - strip
        step_side = pltpu.roll(strip, N - 1, 1) - strip
        squared = step_down * step_down + step_side * step_side + EPS_TV
        inverse = lax.rsqrt(squared)
        flow_down = step_down * inverse
        flow_side = step_side * inverse
        from_up = pltpu.roll(flow_down, 1, 0)[8 : T + 8, :T]
        from_left = pltpu.roll(flow_side, 1, 1)[8 : T + 8, :T]
        from_up = jnp.where((row_id == 0) & (r == 0), zero, from_up)
        from_left = jnp.where((lane_id == 0) & (c == 0), zero, from_left)
        grad_tv = from_up + from_left - (flow_down + flow_side)[8 : T + 8, :T]
        length = (squared * inverse)[8 : T + 8, :T]

        xh, xl = split(x)
        a = mm(lanes(xh, xh, xl), rows(tab("wh"), tab("wl"), tab("wh")))
        ah, al = split(a)
        q = mm(lanes(tab("dh"), tab("dh"), tab("dl")), rows(ah, al, ah))
        mr = q[:N, :T] + q[N:, T:]
        mi = q[:N, T:] - q[N:, :T]
        m_ref[0], m_ref[1] = mr, mi

        def spread(k):
            for i in range(0, T, CH):
                parts = []
                for at in (slice(i, i + CH), slice(T + i, T + i + CH)):
                    m_r, m_i = m_ref[0, at], m_ref[1, at]
                    m_r, m_i = lanes(m_r, m_r), lanes(m_i, m_i)
                    h_r, h_i = hr_ref[k, at], hi_ref[k, at]
                    parts.append((m_r * h_r + m_i * h_i, m_i * h_r - m_r * h_i))
                for j in range(2):
                    at = slice(j * T + i, j * T + i + CH)
                    b_ref[k, 0, at], b_ref[k, 1, at] = split(parts[0][j] + parts[1][j])
                    b_ref[k, 2, at], b_ref[k, 3, at] = split(parts[0][j] - parts[1][j])

        def along_rows(k):
            for n, name in enumerate(("even", "odd")):
                bh, bl = b_ref[k, 2 * n], b_ref[k, 2 * n + 1]
                z = mm(lanes(tab(name + "h"), tab(name + "h"), tab(name + "l")), rows(bh, bl, bh))
                for j in range(2):
                    at = j * T + n * R
                    part = slice(j * T, (j + 1) * T)
                    zh, zl = split(lanes(z[:R, part], z[R:, part]))
                    z_ref[k, at : at + R], z_ref[k, N + at : N + at + R] = zh, zl

        def along_lanes(k, total):
            wi = lanes(tab("wih")[:, :T], tab("wil")[:, :T])
            e = mm(z_ref[k], wi)
            e = (e[:N, :T] + e[:N, T:]) + (e[N:, :T] + e[N:, T:])
            field_ref[k] = e
            square = e * e
            return total + (square[:T] + square[T:])

        intensity = zero
        for step in range(K + 2):
            if 1 <= step <= K:
                along_rows(step - 1)
            if step < K:
                spread(step)
            if step >= 2:
                intensity = along_lanes(step - 2, intensity)
        wanted = rows(target_ref[pl.ds(0, R, stride=2), :], target_ref[pl.ds(1, R, stride=2), :])
        resist = 1.0 / (1.0 + jnp.exp(-SLOPE * (intensity - LEVEL)))
        miss = resist - wanted
        weight = 2.0 * miss * SLOPE * resist * (1.0 - resist)
        term = miss * miss + TV_WEIGHT * length + L1_WEIGHT * jnp.abs(point)
        goal_part[t] = jnp.sum(term.reshape(T // 8, 8, T), axis=0)

        gr_ref[...] = jnp.zeros_like(gr_ref)
        gi_ref[...] = jnp.zeros_like(gi_ref)
        def weigh(k):
            for j in range(2):
                for i in range(0, T, CH):
                    at = slice(j * T + i, j * T + i + CH)
                    v_ref[k, at, :T], v_ref[k, at, T:] = split(weight[i : i + CH] * field_ref[k, at])

        def from_lanes(k):
            wh, wl = tab("wh")[:T], tab("wl")[:T]
            v = v_ref[k]
            y = mm(lanes(v, v), rows(wh, wh, wl, wl))
            for n in range(2):
                for j in range(2):
                    part = slice(j * T, (j + 1) * T)
                    yh, yl = split(lanes(y[n * R : (n + 1) * R, part], y[T + n * R : T + (n + 1) * R, part]))
                    at = j * R
                    y_ref[k, n, at : at + R], y_ref[k, n, T + at : T + at + R] = yh, yl

        def gather(k):
            out = []
            for n in range(2):
                y2 = y_ref[k, n]
                bh = tab("bothh")[:, n * T : (n + 1) * T]
                bl = tab("bothl")[:, n * T : (n + 1) * T]
                out.append(mm(lanes(bh, bh, bl, bl), rows(y2, y2)))
            even, odd = out
            for i in range(0, T, CH):
                parts = [(x[i : i + CH], x[T + i : T + i + CH]) for x in (even, odd)]
                for n, sign in enumerate((1, -1)):
                    at = slice(n * T + i, n * T + i + CH)
                    s_r, s_i = (e + o if sign > 0 else e - o for e, o in zip(*parts))
                    h_r, h_i = hr_ref[k, at], hi_ref[k, at]
                    gr_ref[at] += h_r * s_r - h_i * s_i
                    gi_ref[at] += h_r * s_i + h_i * s_r

        last = t == ITERS - 1
        reducing = None
        if last:
            line = lax.broadcasted_iota(jnp.int32, (8, T), 0)
            value = jnp.zeros((8, T), F32)
            for n in range(ITERS):
                value = jnp.where(line == n, jnp.sum(goal_part[n], axis=0, keepdims=True), value)
            reducing = reduce_start(0, value)
            pending += reducing
        for step in range(K + 2):
            if 1 <= step <= K:
                from_lanes(step - 1)
            if step < K:
                weigh(step)
            if step >= 2:
                gather(step - 2)
        g = lanes(gr_ref[:, :T] + gr_ref[:, T:], gi_ref[:, :T] + gi_ref[:, T:])
        gh, gl = split(g)
        q = mm(lanes(tab("dh"), tab("dh"), tab("dl")), rows(gh, gl, gh))
        z = lanes(q[:N, :T] - q[N:, T:], q[:N, T:] + q[N:, :T])
        zh, zl = split(z)
        g = mm(lanes(zh, zh, zl), rows(tab("wih"), tab("wil"), tab("wih")))
        sent = send_gradient(t, g)
        pending += sent
        if last:
            reducing = reduce_start(1, reduce_end(0, reducing))
            pending += reducing
        for copy in sent:
            copy.wait_recv()
        rows_live = jnp.where(upper, has_up.astype(F32), has_down.astype(F32))
        lanes_live = jnp.where(first_lanes, has_left.astype(F32), has_right.astype(F32))
        below, beside, corner = arrived(2 * t + 1)
        grad_data = 2.0 * (g[:T, :T] + below * rows_live + (beside + corner * rows_live) * lanes_live)
        updated = jnp.clip(
            point - STEP_SIZE * (grad_data + TV_WEIGHT * grad_tv) - STEP_SIZE * L1_WEIGHT, 0.0, 1.0
        )
        if last:
            next_ref[...] = updated
            put(0, next_ref, next_hbm)
            total = reduce_end(1, reducing)
            scale = 1.0 / (size_r * size_c * T * T)
            for n in range(ITERS):
                goal_ref[n] = jnp.sum(total[n : n + 1]) * scale
        else:
            last_ref[...] = updated
            put(1, last_ref, last_hbm)
            point = extrapolate(t + 1, updated, previous)
            previous = updated
            sent = send_point(t + 1, point)
            pending += sent
    for copy in pending:
        copy.wait_send()
    for copy in stored:
        copy.wait()


def shards(size_r, size_c, mask, mask_prev, target, kernels, restart):
    anywhere = pl.BlockSpec(memory_space=pltpu.HBM)
    rows_by, cols_by = factors(size_r, size_c)
    widest = max(rows_by[1] * cols_by[1], rows_by[0] * cols_by[0] * rows_by[2])
    results = pl.pallas_call(
        functools.partial(kernel, size_r, size_c),
        out_shape=(
            jax.ShapeDtypeStruct((T, T), F32),
            jax.ShapeDtypeStruct((T, T), F32),
            jax.ShapeDtypeStruct((ITERS,), F32),
        ),
        in_specs=[anywhere] * 6,
        out_specs=(anywhere, anywhere, pl.BlockSpec(memory_space=pltpu.SMEM)),
        scratch_shapes=[
            pltpu.VMEM((T, T), F32),
            pltpu.VMEM((T, T), F32),
            pltpu.VMEM((T, T), F32),
            pltpu.VMEM((T, T), F32),
            pltpu.VMEM((T, T), F32),
            pltpu.SMEM((1, 1, ITERS), jnp.int32),
            pltpu.VMEM((K, KS, 2, KS), F32),
            pltpu.VMEM(TABLE.shape, BF16),
            pltpu.VMEM((2, KP, N), F32),
            pltpu.VMEM((K, N, N), F32),
            pltpu.VMEM((K, N, N), F32),
            pltpu.VMEM((K, N, T), F32),
            pltpu.VMEM((N, N), F32),
            pltpu.VMEM((N, N), F32),
            pltpu.VMEM((ITERS, T, T), F32),
            pltpu.VMEM((ITERS, T, T), F32),
            pltpu.VMEM((K, 4, N, N), BF16),
            pltpu.VMEM((K, 2 * N, N), BF16),
            pltpu.VMEM((K, N, N), BF16),
            pltpu.VMEM((K, 2, N, N), BF16),
            pltpu.VMEM((2, N, T), F32),
            pltpu.VMEM((2 * ITERS, T, T), F32),
            pltpu.VMEM((2 * ITERS, 2, R, T), F32),
            pltpu.VMEM((2 * ITERS, 2, 2, R // 2, T), F32),
            pltpu.VMEM((2 * ITERS, 2, R, T), F32),
            pltpu.VMEM((2 * ITERS, 2, 2, R // 2, T), F32),
            pltpu.VMEM((ITERS, 8, T), F32),
            pltpu.VMEM((2, widest, 8, T), F32),
            pltpu.VMEM((2, 8, T), F32),
            pltpu.SemaphoreType.DMA((8,)),
            pltpu.SemaphoreType.DMA((2 * ITERS, 8)),
            pltpu.SemaphoreType.DMA((2 * ITERS, 8)),
            pltpu.SemaphoreType.DMA((2, widest)),
            pltpu.SemaphoreType.DMA((2, widest)),
        ],
        compiler_params=pltpu.CompilerParams(
            collective_id=0, has_side_effects=True, vmem_limit_bytes=62 * 1024 * 1024
        ),
        name="fista",
    )(mask, mask_prev, target, jnp.transpose(restart, (1, 2, 0)), jnp.transpose(kernels, (0, 2, 1, 3)), jnp.asarray(TABLE))
    return pl.pallas_call(
        store,
        out_shape=tuple(jax.ShapeDtypeStruct(x.shape, x.dtype) for x in results),
        in_specs=[anywhere] * 3,
        out_specs=(anywhere,) * 3,
        scratch_shapes=[
            pltpu.VMEM((T, T), F32),
            pltpu.VMEM((T, T), F32),
            pltpu.VMEM((ITERS,), F32),
            pltpu.SemaphoreType.DMA((2, 3)),
        ],
        name="store",
    )(*results)


def store(a_hbm, b_hbm, c_hbm, next_hbm, last_hbm, goal_hbm, a_ref, b_ref, c_ref, sems):
    trips = ((a_hbm, a_ref, next_hbm), (b_hbm, b_ref, last_hbm), (c_hbm, c_ref, goal_hbm))
    there = [pltpu.make_async_copy(x, y, sems.at[0, n]) for n, (x, y, _) in enumerate(trips)]
    back = [pltpu.make_async_copy(y, z, sems.at[1, n]) for n, (_, y, z) in enumerate(trips)]
    for copy in there:
        copy.start()
    for first, second in zip(there, back):
        first.wait()
        second.start()
    for copy in back:
        copy.wait()


def solution(mesh):
    in_specs = (P("row", "col"), P("row", "col"), P("row", "col"), P(), P(None, "row", "col"))
    out_specs = (P("row", "col"), P("row", "col"), P())
    body = functools.partial(shards, mesh.shape["row"], mesh.shape["col"])
    return jax.shard_map(body, mesh=mesh, in_specs=in_specs, out_specs=out_specs, check_vma=False)
```

```python
import functools
import math

import jax
import jax.numpy as jnp
import ml_dtypes
import numpy as np
from jax import lax
from jax.experimental import pallas as pl
from jax.experimental.pallas import tpu as pltpu
from jax.sharding import PartitionSpec as P

ITERS = 2
SLOPE = 4.0
LEVEL = 0.8
STEP_SIZE = 0.05
TV_WEIGHT = 0.05
L1_WEIGHT = 0.5
EPS_TV = 0.01
PRIOR_STEPS = 10.0

T = 128
N = 256
KS = 129
KP = 144
K = 8
R = 64
CH = 16
MESH = pl.DeviceIdType.MESH
F32 = jnp.float32
BF16 = jnp.bfloat16


def tables():
    pos = np.arange(N)
    shift = np.where(pos < T + R, pos, pos - N).astype(np.float64)
    tap = np.arange(N) - R
    alive = (np.arange(N) < KS).astype(np.float64)
    freq2 = np.arange(T) + 0.5
    freq1 = np.arange(N)
    step = 2.0 * math.pi / N

    def right(offset):
        phase = offset[:, None] * freq2[None, :] * step
        return np.concatenate([np.cos(phase), -np.sin(phase)], axis=1)

    def left(offset):
        phase = freq1[:, None] * offset[None, :] * step
        return np.concatenate([np.cos(phase), np.sin(phase)], axis=0)

    w = right(shift)
    wk = right(tap) * alive[:, None]
    d = left(pos)
    dk = left(tap) * alive[None, :]
    wi = w.T * (2.0 / (N * N))

    def half(odd):
        rows = 2 * np.arange(T // 2) + odd
        phase = rows[:, None] * np.arange(T)[None, :] * step
        c, s = np.cos(phase), np.sin(phase)
        return np.concatenate([np.concatenate([c, -s], 1), np.concatenate([s, c], 1)], 0)

    even, odd = half(0), half(1)
    both = np.concatenate([even.T, odd.T], axis=1)
    place, parts, row = {}, [], 0
    for name, table in (("w", w), ("wk", wk), ("d", d), ("dk", dk), ("even", even), ("odd", odd), ("both", both), ("wi", wi)):
        high = table.astype(np.float32).astype(ml_dtypes.bfloat16)
        low = (table - high.astype(np.float64)).astype(np.float32).astype(ml_dtypes.bfloat16)
        for which, part in (("h", high), ("l", low)):
            place[name + which] = (row, row + part.shape[0])
            parts.append(part)
            row += part.shape[0]
    return place, np.concatenate(parts, axis=0)


PLACE, TABLE = tables()


def factors(size_r, size_c):
    core = math.gcd(size_r, 2)
    x = math.gcd(size_r // core, 4)
    y = math.gcd(size_c, 4)
    return (size_r // (core * x), x, core), (size_c // y, y)


def split(x):
    high = x.astype(BF16)
    return high, (x - high.astype(F32)).astype(BF16)


def mm(a, b):
    return jnp.dot(a, b, preferred_element_type=F32)


def rows(*parts):
    return jnp.concatenate(parts, axis=0)


def lanes(*parts):
    return jnp.concatenate(parts, axis=1)


def kernel(
    size_r,
    size_c,
    mask_hbm,
    prev_hbm,
    target_hbm,
    restart_hbm,
    taps_hbm,
    table_hbm,
    next_hbm,
    last_hbm,
    goal_ref,
    next_ref,
    last_ref,
    mask_ref,
    prev_ref,
    target_ref,
    restart_ref,
    taps_ref,
    table_ref,
    padded_ref,
    hr_ref,
    hi_ref,
    field_ref,
    gr_ref,
    gi_ref,
    point_ref,
    own_ref,
    b_ref,
    z_ref,
    v_ref,
    y_ref,
    m_ref,
    ud_ref,
    side_ref,
    corner_ref,
    side_out,
    corner_out,
    goal_part,
    slots_ref,
    sums_ref,
    local_sem,
    send_sem,
    recv_sem,
    red_send,
    red_recv,
):
    r = lax.axis_index("row")
    c = lax.axis_index("col")
    near = {}
    for dr in (-1, 0, 1):
        for dc in (-1, 0, 1):
            if dr or dc:
                near[dr, dc] = (lax.rem(r + dr + size_r, size_r), lax.rem(c + dc + size_c, size_c))
    rows_by, cols_by = factors(size_r, size_c)
    z_high, x, core = r // (rows_by[1] * rows_by[2]), lax.rem(r // rows_by[2], rows_by[1]), lax.rem(r, rows_by[2])
    z_low, y = c // cols_by[1], lax.rem(c, cols_by[1])

    def device(z_high, x, core, z_low, y):
        return (z_high * rows_by[1] + x) * rows_by[2] + core, z_low * cols_by[1] + y

    groups = []
    peers = []
    for i in range(rows_by[1]):
        for j in range(cols_by[1]):
            if i or j:
                peers.append(device(z_high, lax.rem(x + i, rows_by[1]), core, z_low, lax.rem(y + j, cols_by[1])))
    groups.append((x * cols_by[1] + y, peers))
    peers = []
    for i in range(rows_by[0]):
        for j in range(cols_by[0]):
            for k in range(rows_by[2]):
                if i or j or k:
                    peers.append(
                        device(
                            lax.rem(z_high + i, rows_by[0]), x, lax.rem(core + k, rows_by[2]), lax.rem(z_low + j, cols_by[0]), y
                        )
                    )
    groups.append(((z_high * cols_by[0] + z_low) * rows_by[2] + core, peers))

    def tab(name):
        first, end = PLACE[name]
        return table_ref[first:end, :]

    loads = []
    for n, (source, target) in enumerate(
        (
            (mask_hbm, mask_ref),
            (prev_hbm, prev_ref),
            (restart_hbm, restart_ref),
            (table_hbm, table_ref),
            (taps_hbm, taps_ref),
            (target_hbm, target_ref),
        )
    ):
        copy = pltpu.make_async_copy(source, target, local_sem.at[n])
        loads.append(copy)
    for copy in loads[:3]:
        copy.start()
    barrier = pltpu.get_barrier_semaphore()
    everyone = list(near.values()) + [peer for _, peers in groups for peer in peers]
    for peer in everyone:
        pl.semaphore_signal(barrier, inc=1, device_id=peer, device_id_type=MESH)
    for copy in loads[3:]:
        copy.start()

    stored = []

    def put(n, source, target):
        copy = pltpu.make_async_copy(source, target, local_sem.at[6 + n])
        copy.start()
        stored.append(copy)

    def extrapolate(t, current, previous):
        momentum = (t + PRIOR_STEPS - 1.0) / (t + PRIOR_STEPS + 2.0)
        keep = 1.0 - restart_ref[0, 0, t].astype(F32)
        point = current + keep * momentum * (current - previous)
        point_ref[t] = point
        return point

    def start(slot, n, dr, dc, source, target):
        copy = pltpu.make_async_remote_copy(
            src_ref=source,
            dst_ref=target,
            send_sem=send_sem.at[slot, n],
            recv_sem=recv_sem.at[slot, n],
            device_id=near[dr, dc],
            device_id_type=MESH,
        )
        copy.start()
        return copy

    def send_corners(slot, sign, block):
        ways = (-sign, sign)
        for h in range(2):
            corner_out[slot, h, 0], corner_out[slot, h, 1] = pack(block[h * R : (h + 1) * R])
        copies = []
        for h, p in ((1, 1), (0, 0), (1, 0), (0, 1)):
            copies.append(
                start(slot, 2 * h + p, ways[h], ways[p], corner_out.at[slot, h, p], corner_ref.at[slot, h, p])
            )
        return copies

    def send_beyond(slot, sign, ref):
        ways = (-sign, sign)
        halves = [pl.ds(h * R, R) for h in range(2)]
        return [start(slot, 4 + h, ways[h], 0, ref.at[halves[h]], ud_ref.at[slot, halves[h]]) for h in range(2)]

    def send_beside(slot, sign, block):
        ways = (-sign, sign)
        copies = []
        for p, part in enumerate(pack(block)):
            side_out[slot, p] = part
            copies.append(start(slot, 6 + p, 0, ways[p], side_out.at[slot, p], side_ref.at[slot, p]))
        return copies

    def pack(block):
        half = block.shape[0] // 2
        turned = pltpu.roll(block, R, 1)
        first = first_lanes[:half]
        return jnp.where(first, block[:half], turned[half:]), jnp.where(first, turned[:half], block[half:])

    def unpack(low, high):
        first = first_lanes[: low.shape[0]]
        return rows(jnp.where(first, low, pltpu.roll(high, R, 1)), jnp.where(first, pltpu.roll(low, R, 1), high))

    def arrived(slot, copies):
        for copy in copies:
            copy.wait_recv()
        return ud_ref[slot], unpack(side_ref[slot, 0], side_ref[slot, 1])

    def arrived_corners(slot, copies):
        for copy in copies:
            copy.wait_recv()
        return rows(*(unpack(corner_ref[slot, h, 0], corner_ref[slot, h, 1]) for h in range(2)))

    def send_point(t, point):
        near_by = send_corners(2 * t, 1, point)
        return near_by, send_beyond(2 * t, 1, point_ref.at[t]) + send_beside(2 * t, 1, point)

    def reduce_start(phase, value):
        me, peers = groups[phase]
        slots_ref[phase, me] = value
        sums_ref[phase] = value
        copies = []
        for d, peer in enumerate(peers):
            copy = pltpu.make_async_remote_copy(
                src_ref=sums_ref.at[phase],
                dst_ref=slots_ref.at[phase, me],
                send_sem=red_send.at[phase, d],
                recv_sem=red_recv.at[phase, d],
                device_id=peer,
                device_id_type=MESH,
            )
            copy.start()
            copies.append(copy)
        return copies

    def reduce_end(phase, copies):
        for copy in copies:
            copy.wait_recv()
        total = slots_ref[phase, 0]
        for n in range(1, len(copies) + 1):
            total = total + slots_ref[phase, n]
        return total

    row_id = lax.broadcasted_iota(jnp.int32, (T, T), 0)
    lane_id = lax.broadcasted_iota(jnp.int32, (T, T), 1)
    upper = row_id < R
    first_lanes = lane_id < R
    has_up, has_down = r > 0, r < size_r - 1
    has_left, has_right = c > 0, c < size_c - 1

    for copy in loads[:3]:
        copy.wait()
    point = extrapolate(0, mask_ref[...], prev_ref[...])
    pl.semaphore_wait(barrier, len(everyone))
    sent = send_point(0, point)
    pending = sent[0] + sent[1]

    padded_ref[...] = jnp.zeros_like(padded_ref)
    for copy in loads[3:]:
        copy.wait()

    def spectrum(k, carry):
        for part in range(2):
            padded_ref[part, 0:KS, 0:KS] = taps_ref[k, :, part, :]
            xh, xl = split(padded_ref[part])
            y = mm(lanes(xh, xh, xl), rows(tab("wkh"), tab("wkl"), tab("wkh")))
            yh, yl = split(y)
            dh, dl = tab("dkh")[:, :KP], tab("dkl")[:, :KP]
            q = mm(dh, yh) + mm(dh, yl) + mm(dl, yh)
            hr_ref[k, :, part * T : (part + 1) * T] = q[:N, :T] + q[N:, T:]
            hi_ref[k, :, part * T : (part + 1) * T] = q[:N, T:] - q[N:, :T]
        return carry

    lax.fori_loop(0, K, spectrum, 0, unroll=True)

    previous = mask_ref[...]
    objective = []
    for t in range(ITERS):
        zero = jnp.zeros((T, T), F32)
        rows_live = jnp.where(upper, has_down.astype(F32), has_up.astype(F32))
        lanes_live = jnp.where(first_lanes, has_right.astype(F32), has_left.astype(F32))
        below, beside = arrived(2 * t, sent[1])
        below = below * rows_live
        beside = beside * lanes_live
        corner = arrived_corners(2 * t, sent[0]) * (rows_live * lanes_live)
        xh, xl = split(rows(lanes(point, beside), lanes(below, corner)))
        a = mm(lanes(xh, xh, xl), rows(tab("wh"), tab("wl"), tab("wh")))
        ah, al = split(a)
        q = mm(lanes(tab("dh"), tab("dh"), tab("dl")), rows(ah, al, ah))
        m_ref[0] = q[:N, :T] + q[N:, T:]
        m_ref[1] = q[:N, T:] - q[N:, :T]
        x = rows(lanes(point, beside), lanes(below, corner))

        strip = rows(x[N - 8 :], x[: T + 8])
        high_rows = strip.shape[0]
        step_down = pltpu.roll(strip, high_rows - 1, 0) - strip
        step_side = pltpu.roll(strip, N - 1, 1) - strip
        squared = step_down * step_down + step_side * step_side + EPS_TV
        inverse = lax.rsqrt(squared)
        flow_down = step_down * inverse
        flow_side = step_side * inverse
        from_up = pltpu.roll(flow_down, 1, 0)[8 : T + 8, :T]
        from_left = pltpu.roll(flow_side, 1, 1)[8 : T + 8, :T]
        from_up = jnp.where((row_id == 0) & (r == 0), zero, from_up)
        from_left = jnp.where((lane_id == 0) & (c == 0), zero, from_left)
        grad_tv = from_up + from_left - (flow_down + flow_side)[8 : T + 8, :T]
        length = (squared * inverse)[8 : T + 8, :T]

        def spread(k):
            for i in range(0, T, CH):
                parts = []
                for at in (slice(i, i + CH), slice(T + i, T + i + CH)):
                    m_r, m_i = m_ref[0, at], m_ref[1, at]
                    m_r, m_i = lanes(m_r, m_r), lanes(m_i, m_i)
                    h_r, h_i = hr_ref[k, at], hi_ref[k, at]
                    parts.append((m_r * h_r + m_i * h_i, m_i * h_r - m_r * h_i))
                for j in range(2):
                    at = slice(j * T + i, j * T + i + CH)
                    b_ref[k, 0, at], b_ref[k, 1, at] = split(parts[0][j] + parts[1][j])
                    b_ref[k, 2, at], b_ref[k, 3, at] = split(parts[0][j] - parts[1][j])

        def along_rows(k):
            for n, name in enumerate(("even", "odd")):
                bh, bl = b_ref[k, 2 * n], b_ref[k, 2 * n + 1]
                z = mm(lanes(tab(name + "h"), tab(name + "h"), tab(name + "l")), rows(bh, bl, bh))
                for j in range(2):
                    at = j * T + n * R
                    part = slice(j * T, (j + 1) * T)
                    zh, zl = split(lanes(z[:R, part], z[R:, part]))
                    z_ref[k, at : at + R], z_ref[k, N + at : N + at + R] = zh, zl

        def along_lanes(k, total):
            wi = lanes(tab("wih")[:, :T], tab("wil")[:, :T])
            e = mm(z_ref[k], wi)
            e = (e[:N, :T] + e[:N, T:]) + (e[N:, :T] + e[N:, T:])
            field_ref[k] = e
            square = e * e
            return total + (square[:T] + square[T:])

        intensity = zero
        for step in range(K + 2):
            if 1 <= step <= K:
                along_rows(step - 1)
            if step < K:
                spread(step)
            if step >= 2:
                intensity = along_lanes(step - 2, intensity)
        wanted = rows(target_ref[pl.ds(0, R, stride=2), :], target_ref[pl.ds(1, R, stride=2), :])
        resist = 1.0 / (1.0 + jnp.exp(-SLOPE * (intensity - LEVEL)))
        miss = resist - wanted
        weight = 2.0 * miss * SLOPE * resist * (1.0 - resist)
        term = miss * miss + TV_WEIGHT * length + L1_WEIGHT * jnp.abs(point)
        goal_part[t] = jnp.sum(term.reshape(T // 8, 8, T), axis=0)

        gr_ref[...] = jnp.zeros_like(gr_ref)
        gi_ref[...] = jnp.zeros_like(gi_ref)
        def weigh(k):
            for j in range(2):
                for i in range(0, T, CH):
                    at = slice(j * T + i, j * T + i + CH)
                    v_ref[k, at, :T], v_ref[k, at, T:] = split(weight[i : i + CH] * field_ref[k, at])

        def from_lanes(k):
            wh, wl = tab("wh")[:T], tab("wl")[:T]
            v = v_ref[k]
            y = mm(lanes(v, v), rows(wh, wh, wl, wl))
            for n in range(2):
                for j in range(2):
                    part = slice(j * T, (j + 1) * T)
                    yh, yl = split(lanes(y[n * R : (n + 1) * R, part], y[T + n * R : T + (n + 1) * R, part]))
                    at = j * R
                    y_ref[k, n, at : at + R], y_ref[k, n, T + at : T + at + R] = yh, yl

        def gather(k):
            out = []
            for n in range(2):
                y2 = y_ref[k, n]
                bh = tab("bothh")[:, n * T : (n + 1) * T]
                bl = tab("bothl")[:, n * T : (n + 1) * T]
                out.append(mm(lanes(bh, bh, bl, bl), rows(y2, y2)))
            even, odd = out
            for i in range(0, T, CH):
                parts = [(x[i : i + CH], x[T + i : T + i + CH]) for x in (even, odd)]
                for n, sign in enumerate((1, -1)):
                    at = slice(n * T + i, n * T + i + CH)
                    s_r, s_i = (e + o if sign > 0 else e - o for e, o in zip(*parts))
                    h_r, h_i = hr_ref[k, at], hi_ref[k, at]
                    gr_ref[at] += h_r * s_r - h_i * s_i
                    gi_ref[at] += h_r * s_i + h_i * s_r

        last = t == ITERS - 1
        reducing = None
        if last:
            parts = [jnp.sum(goal_part[n], axis=0, keepdims=True) for n in range(ITERS)]
            parts = [part + pltpu.roll(part, R, 1) for part in parts]
            value = jnp.where(first_lanes[:1], parts[0], parts[1])
            reducing = reduce_start(0, value)
            pending += reducing
        for step in range(K + 2):
            if 1 <= step <= K:
                from_lanes(step - 1)
            if step < K:
                weigh(step)
            if step >= 2:
                gather(step - 2)
        g = lanes(gr_ref[:, :T] + gr_ref[:, T:], gi_ref[:, :T] + gi_ref[:, T:])
        gh, gl = split(g)

        def back(at):
            dh, dl = (rows(tab(name)[at : at + T], tab(name)[N + at : N + at + T]) for name in ("dh", "dl"))
            q = mm(lanes(dh, dh, dl), rows(gh, gl, gh))
            zh, zl = split(lanes(q[:T, :T] - q[T:, T:], q[:T, T:] + q[T:, :T]))
            return mm(lanes(zh, zh, zl), rows(tab("wih"), tab("wil"), tab("wih")))

        slot = 2 * t + 1
        halo = back(T)
        sent_corners = send_corners(slot, -1, halo[:, T:])
        own_ref[t] = halo[:, :T]
        sent = send_beyond(slot, -1, own_ref.at[t])
        g = back(0)
        sent += send_beside(slot, -1, g[:, T:])
        pending += sent_corners + sent
        if last:
            reducing = reduce_start(1, reduce_end(0, reducing))
            pending += reducing
        rows_live = jnp.where(upper, has_up.astype(F32), has_down.astype(F32))
        lanes_live = jnp.where(first_lanes, has_left.astype(F32), has_right.astype(F32))
        below, beside = arrived(slot, sent)
        grad_data = g[:, :T] + below * rows_live + beside * lanes_live
        corner = arrived_corners(slot, sent_corners)
        grad_data = 2.0 * (grad_data + corner * (rows_live * lanes_live))
        updated = jnp.clip(
            point - STEP_SIZE * (grad_data + TV_WEIGHT * grad_tv) - STEP_SIZE * L1_WEIGHT, 0.0, 1.0
        )
        if last:
            next_ref[...] = updated
            put(0, next_ref, next_hbm)
            total = reduce_end(1, reducing)
            scale = 1.0 / (size_r * size_c * T * T)
            for n in range(ITERS):
                goal_ref[n] = jnp.sum(jnp.where((lane_id[:1] < R) == (n == 0), total, 0.0)) * scale
        else:
            last_ref[...] = updated
            put(1, last_ref, last_hbm)
            point = extrapolate(t + 1, updated, previous)
            previous = updated
            sent = send_point(t + 1, point)
            pending += sent[0] + sent[1]
    for copy in pending:
        copy.wait_send()
    for copy in stored:
        copy.wait()


def shards(size_r, size_c, mask, mask_prev, target, kernels, restart):
    anywhere = pl.BlockSpec(memory_space=pltpu.HBM)
    rows_by, cols_by = factors(size_r, size_c)
    widest = max(rows_by[1] * cols_by[1], rows_by[0] * cols_by[0] * rows_by[2])
    results = pl.pallas_call(
        functools.partial(kernel, size_r, size_c),
        out_shape=(
            jax.ShapeDtypeStruct((T, T), F32),
            jax.ShapeDtypeStruct((T, T), F32),
            jax.ShapeDtypeStruct((ITERS,), F32),
        ),
        in_specs=[anywhere] * 6,
        out_specs=(anywhere, anywhere, pl.BlockSpec(memory_space=pltpu.SMEM)),
        scratch_shapes=[
            pltpu.VMEM((T, T), F32),
            pltpu.VMEM((T, T), F32),
            pltpu.VMEM((T, T), F32),
            pltpu.VMEM((T, T), F32),
            pltpu.VMEM((T, T), F32),
            pltpu.SMEM((1, 1, ITERS), jnp.int32),
            pltpu.VMEM((K, KS, 2, KS), F32),
            pltpu.VMEM(TABLE.shape, BF16),
            pltpu.VMEM((2, KP, N), F32),
            pltpu.VMEM((K, N, N), F32),
            pltpu.VMEM((K, N, N), F32),
            pltpu.VMEM((K, N, T), F32),
            pltpu.VMEM((N, N), F32),
            pltpu.VMEM((N, N), F32),
            pltpu.VMEM((ITERS, T, T), F32),
            pltpu.VMEM((ITERS, T, T), F32),
            pltpu.VMEM((K, 4, N, N), BF16),
            pltpu.VMEM((K, 2 * N, N), BF16),
            pltpu.VMEM((K, N, N), BF16),
            pltpu.VMEM((K, 2, N, N), BF16),
            pltpu.VMEM((2, N, T), F32),
            pltpu.VMEM((2 * ITERS, T, T), F32),
            pltpu.VMEM((2 * ITERS, 2, R, T), F32),
            pltpu.VMEM((2 * ITERS, 2, 2, R // 2, T), F32),
            pltpu.VMEM((2 * ITERS, 2, R, T), F32),
            pltpu.VMEM((2 * ITERS, 2, 2, R // 2, T), F32),
            pltpu.VMEM((ITERS, 8, T), F32),
            pltpu.VMEM((2, widest, 1, T), F32),
            pltpu.VMEM((2, 1, T), F32),
            pltpu.SemaphoreType.DMA((8,)),
            pltpu.SemaphoreType.DMA((2 * ITERS, 8)),
            pltpu.SemaphoreType.DMA((2 * ITERS, 8)),
            pltpu.SemaphoreType.DMA((2, widest)),
            pltpu.SemaphoreType.DMA((2, widest)),
        ],
        compiler_params=pltpu.CompilerParams(
            collective_id=0, has_side_effects=True, vmem_limit_bytes=62 * 1024 * 1024
        ),
        name="fista",
    )(mask, mask_prev, target, jnp.transpose(restart, (1, 2, 0)), jnp.transpose(kernels, (0, 2, 1, 3)), jnp.asarray(TABLE))
    return pl.pallas_call(
        store,
        out_shape=tuple(jax.ShapeDtypeStruct(x.shape, x.dtype) for x in results),
        in_specs=[anywhere] * 3,
        out_specs=(anywhere,) * 3,
        scratch_shapes=[
            pltpu.VMEM((T, T), F32),
            pltpu.VMEM((T, T), F32),
            pltpu.VMEM((ITERS,), F32),
            pltpu.SemaphoreType.DMA((2, 3)),
        ],
        name="store",
    )(*results)


def store(a_hbm, b_hbm, c_hbm, next_hbm, last_hbm, goal_hbm, a_ref, b_ref, c_ref, sems):
    trips = ((a_hbm, a_ref, next_hbm), (b_hbm, b_ref, last_hbm), (c_hbm, c_ref, goal_hbm))
    there = [pltpu.make_async_copy(x, y, sems.at[0, n]) for n, (x, y, _) in enumerate(trips)]
    back = [pltpu.make_async_copy(y, z, sems.at[1, n]) for n, (_, y, z) in enumerate(trips)]
    for copy in there:
        copy.start()
    for first, second in zip(there, back):
        first.wait()
        second.start()
    for copy in back:
        copy.wait()


def solution(mesh):
    in_specs = (P("row", "col"), P("row", "col"), P("row", "col"), P(), P(None, "row", "col"))
    out_specs = (P("row", "col"), P("row", "col"), P())
    body = functools.partial(shards, mesh.shape["row"], mesh.shape["col"])
    return jax.shard_map(body, mesh=mesh, in_specs=in_specs, out_specs=out_specs, check_vma=False)
```

```python
import functools
import math

import jax
import jax.numpy as jnp
import ml_dtypes
import numpy as np
from jax import lax
from jax.experimental import pallas as pl
from jax.experimental.pallas import tpu as pltpu
from jax.sharding import PartitionSpec as P

ITERS = 2
SLOPE = 4.0
LEVEL = 0.8
STEP_SIZE = 0.05
TV_WEIGHT = 0.05
L1_WEIGHT = 0.5
EPS_TV = 0.01
PRIOR_STEPS = 10.0

T = 128
N = 256
KS = 129
KP = 144
K = 8
R = 64
CH = 16
MESH = pl.DeviceIdType.MESH
F32 = jnp.float32
BF16 = jnp.bfloat16


def tables():
    pos = np.arange(N)
    shift = np.where(pos < T + R, pos, pos - N).astype(np.float64)
    tap = np.arange(N) - R
    alive = (np.arange(N) < KS).astype(np.float64)
    freq2 = np.arange(T) + 0.5
    freq1 = np.arange(N)
    step = 2.0 * math.pi / N

    def right(offset):
        phase = offset[:, None] * freq2[None, :] * step
        return np.concatenate([np.cos(phase), -np.sin(phase)], axis=1)

    def left(offset):
        phase = freq1[:, None] * offset[None, :] * step
        return np.concatenate([np.cos(phase), np.sin(phase)], axis=0)

    w = right(shift)
    wk = right(tap) * alive[:, None]
    d = left(pos)
    dk = left(tap) * alive[None, :]
    wi = w.T * (2.0 / (N * N))

    def half(odd):
        rows = 2 * np.arange(T // 2) + odd
        phase = rows[:, None] * np.arange(T)[None, :] * step
        c, s = np.cos(phase), np.sin(phase)
        return np.concatenate([np.concatenate([c, -s], 1), np.concatenate([s, c], 1)], 0)

    even, odd = half(0), half(1)
    both = np.concatenate([even.T, odd.T], axis=1)
    place, parts, row = {}, [], 0
    for name, table in (("w", w), ("wk", wk), ("d", d), ("dk", dk), ("even", even), ("odd", odd), ("both", both), ("wi", wi)):
        high = table.astype(np.float32).astype(ml_dtypes.bfloat16)
        low = (table - high.astype(np.float64)).astype(np.float32).astype(ml_dtypes.bfloat16)
        for which, part in (("h", high), ("l", low)):
            place[name + which] = (row, row + part.shape[0])
            parts.append(part)
            row += part.shape[0]
    return place, np.concatenate(parts, axis=0)


PLACE, TABLE = tables()


def factors(size_r, size_c):
    core = math.gcd(size_r, 2)
    x = math.gcd(size_r // core, 4)
    y = math.gcd(size_c, 4)
    return (size_r // (core * x), x, core), (size_c // y, y)


def split(x):
    high = x.astype(BF16)
    return high, (x - high.astype(F32)).astype(BF16)


def mm(a, b):
    return jnp.dot(a, b, preferred_element_type=F32)


def rows(*parts):
    return jnp.concatenate(parts, axis=0)


def lanes(*parts):
    return jnp.concatenate(parts, axis=1)


def kernel(
    size_r,
    size_c,
    mask_hbm,
    prev_hbm,
    target_hbm,
    restart_hbm,
    taps_hbm,
    table_hbm,
    next_hbm,
    last_hbm,
    goal_ref,
    next_ref,
    last_ref,
    mask_ref,
    prev_ref,
    target_ref,
    restart_ref,
    taps_ref,
    table_ref,
    padded_ref,
    hr_ref,
    hi_ref,
    field_ref,
    gr_ref,
    gi_ref,
    point_ref,
    own_ref,
    b_ref,
    z_ref,
    v_ref,
    y_ref,
    m_ref,
    ud_ref,
    side_ref,
    corner_ref,
    side_out,
    corner_out,
    goal_part,
    slots_ref,
    sums_ref,
    local_sem,
    send_sem,
    recv_sem,
    red_send,
    red_recv,
):
    r = lax.axis_index("row")
    c = lax.axis_index("col")
    near = {}
    for dr in (-1, 0, 1):
        for dc in (-1, 0, 1):
            if dr or dc:
                near[dr, dc] = (lax.rem(r + dr + size_r, size_r), lax.rem(c + dc + size_c, size_c))
    rows_by, cols_by = factors(size_r, size_c)
    z_high, x, core = r // (rows_by[1] * rows_by[2]), lax.rem(r // rows_by[2], rows_by[1]), lax.rem(r, rows_by[2])
    z_low, y = c // cols_by[1], lax.rem(c, cols_by[1])

    def device(z_high, x, core, z_low, y):
        return (z_high * rows_by[1] + x) * rows_by[2] + core, z_low * cols_by[1] + y

    groups = []
    peers = []
    for i in range(rows_by[1]):
        for j in range(cols_by[1]):
            if i or j:
                peers.append(device(z_high, lax.rem(x + i, rows_by[1]), core, z_low, lax.rem(y + j, cols_by[1])))
    groups.append((x * cols_by[1] + y, peers))
    peers = []
    for i in range(rows_by[0]):
        for j in range(cols_by[0]):
            for k in range(rows_by[2]):
                if i or j or k:
                    peers.append(
                        device(
                            lax.rem(z_high + i, rows_by[0]), x, lax.rem(core + k, rows_by[2]), lax.rem(z_low + j, cols_by[0]), y
                        )
                    )
    groups.append(((z_high * cols_by[0] + z_low) * rows_by[2] + core, peers))

    groups.reverse()

    def tab(name):
        first, end = PLACE[name]
        return table_ref[first:end, :]

    loads = []
    for n, (source, target) in enumerate(
        (
            (mask_hbm, mask_ref),
            (prev_hbm, prev_ref),
            (restart_hbm, restart_ref),
            (table_hbm, table_ref),
            (taps_hbm, taps_ref),
            (target_hbm, target_ref),
        )
    ):
        copy = pltpu.make_async_copy(source, target, local_sem.at[n])
        loads.append(copy)
    for copy in loads[:3]:
        copy.start()
    barrier = pltpu.get_barrier_semaphore()
    everyone = list(near.values()) + [peer for _, peers in groups for peer in peers]
    for peer in everyone:
        pl.semaphore_signal(barrier, inc=1, device_id=peer, device_id_type=MESH)
    for copy in loads[3:]:
        copy.start()

    stored = []

    def put(n, source, target):
        copy = pltpu.make_async_copy(source, target, local_sem.at[6 + n])
        copy.start()
        stored.append(copy)

    def extrapolate(t, current, previous):
        momentum = (t + PRIOR_STEPS - 1.0) / (t + PRIOR_STEPS + 2.0)
        keep = 1.0 - restart_ref[0, 0, t].astype(F32)
        point = current + keep * momentum * (current - previous)
        point_ref[t] = point
        return point

    def start(slot, n, dr, dc, source, target):
        copy = pltpu.make_async_remote_copy(
            src_ref=source,
            dst_ref=target,
            send_sem=send_sem.at[slot, n],
            recv_sem=recv_sem.at[slot, n],
            device_id=near[dr, dc],
            device_id_type=MESH,
        )
        copy.start()
        return copy

    def send_corners(slot, sign, block):
        ways = (-sign, sign)
        for h in range(2):
            corner_out[slot, h, 0], corner_out[slot, h, 1] = pack(block[h * R : (h + 1) * R])
        copies = []
        for h, p in ((1, 1), (0, 0), (1, 0), (0, 1)):
            copies.append(
                start(slot, 2 * h + p, ways[h], ways[p], corner_out.at[slot, h, p], corner_ref.at[slot, h, p])
            )
        return copies

    def send_beyond(slot, sign, ref):
        ways = (-sign, sign)
        halves = [pl.ds(h * R, R) for h in range(2)]
        return [start(slot, 4 + h, ways[h], 0, ref.at[halves[h]], ud_ref.at[slot, halves[h]]) for h in range(2)]

    def send_beside(slot, sign, block):
        ways = (-sign, sign)
        copies = []
        for p, part in enumerate(pack(block)):
            side_out[slot, p] = part
            copies.append(start(slot, 6 + p, 0, ways[p], side_out.at[slot, p], side_ref.at[slot, p]))
        return copies

    def pack(block):
        half = block.shape[0] // 2
        turned = pltpu.roll(block, R, 1)
        first = first_lanes[:half]
        return jnp.where(first, block[:half], turned[half:]), jnp.where(first, turned[:half], block[half:])

    def unpack(low, high):
        first = first_lanes[: low.shape[0]]
        return rows(jnp.where(first, low, pltpu.roll(high, R, 1)), jnp.where(first, pltpu.roll(low, R, 1), high))

    def arrived(slot, copies):
        for copy in copies:
            copy.wait_recv()
        return ud_ref[slot], unpack(side_ref[slot, 0], side_ref[slot, 1])

    def arrived_corners(slot, copies):
        for copy in copies:
            copy.wait_recv()
        return rows(*(unpack(corner_ref[slot, h, 0], corner_ref[slot, h, 1]) for h in range(2)))

    def send_point(t, point):
        near_by = send_corners(2 * t, 1, point)
        return near_by, send_beyond(2 * t, 1, point_ref.at[t]) + send_beside(2 * t, 1, point)

    def reduce_start(phase, value):
        me, peers = groups[phase]
        slots_ref[phase, me] = value
        sums_ref[phase] = value
        copies = []
        for d, peer in enumerate(peers):
            copy = pltpu.make_async_remote_copy(
                src_ref=sums_ref.at[phase],
                dst_ref=slots_ref.at[phase, me],
                send_sem=red_send.at[phase, d],
                recv_sem=red_recv.at[phase, d],
                device_id=peer,
                device_id_type=MESH,
            )
            copy.start()
            copies.append(copy)
        return copies

    def reduce_end(phase, copies):
        for copy in copies:
            copy.wait_recv()
        total = slots_ref[phase, 0]
        for n in range(1, len(copies) + 1):
            total = total + slots_ref[phase, n]
        return total

    row_id = lax.broadcasted_iota(jnp.int32, (T, T), 0)
    lane_id = lax.broadcasted_iota(jnp.int32, (T, T), 1)
    upper = row_id < R
    first_lanes = lane_id < R
    has_up, has_down = r > 0, r < size_r - 1
    has_left, has_right = c > 0, c < size_c - 1

    for copy in loads[:3]:
        copy.wait()
    point = extrapolate(0, mask_ref[...], prev_ref[...])
    pl.semaphore_wait(barrier, len(everyone))
    sent = send_point(0, point)
    pending = sent[0] + sent[1]

    padded_ref[...] = jnp.zeros_like(padded_ref)
    for copy in loads[3:]:
        copy.wait()

    def spectrum(k, carry):
        for part in range(2):
            padded_ref[part, 0:KS, 0:KS] = taps_ref[k, :, part, :]
            xh, xl = split(padded_ref[part])
            y = mm(lanes(xh, xh, xl), rows(tab("wkh"), tab("wkl"), tab("wkh")))
            yh, yl = split(y)
            dh, dl = tab("dkh")[:, :KP], tab("dkl")[:, :KP]
            q = mm(dh, yh) + mm(dh, yl) + mm(dl, yh)
            hr_ref[k, :, part * T : (part + 1) * T] = q[:N, :T] + q[N:, T:]
            hi_ref[k, :, part * T : (part + 1) * T] = q[:N, T:] - q[N:, :T]
        return carry

    lax.fori_loop(0, K, spectrum, 0, unroll=True)

    previous = mask_ref[...]
    objective = []
    for t in range(ITERS):
        zero = jnp.zeros((T, T), F32)
        rows_live = jnp.where(upper, has_down.astype(F32), has_up.astype(F32))
        lanes_live = jnp.where(first_lanes, has_right.astype(F32), has_left.astype(F32))
        below, beside = arrived(2 * t, sent[1])
        below = below * rows_live
        beside = beside * lanes_live
        corner = arrived_corners(2 * t, sent[0]) * (rows_live * lanes_live)
        xh, xl = split(rows(lanes(point, beside), lanes(below, corner)))
        a = mm(lanes(xh, xh, xl), rows(tab("wh"), tab("wl"), tab("wh")))
        ah, al = split(a)
        q = mm(lanes(tab("dh"), tab("dh"), tab("dl")), rows(ah, al, ah))
        m_ref[0] = q[:N, :T] + q[N:, T:]
        m_ref[1] = q[:N, T:] - q[N:, :T]
        x = rows(lanes(point, beside), lanes(below, corner))

        strip = rows(x[N - 8 :], x[: T + 8])
        high_rows = strip.shape[0]
        step_down = pltpu.roll(strip, high_rows - 1, 0) - strip
        step_side = pltpu.roll(strip, N - 1, 1) - strip
        squared = step_down * step_down + step_side * step_side + EPS_TV
        inverse = lax.rsqrt(squared)
        flow_down = step_down * inverse
        flow_side = step_side * inverse
        from_up = pltpu.roll(flow_down, 1, 0)[8 : T + 8, :T]
        from_left = pltpu.roll(flow_side, 1, 1)[8 : T + 8, :T]
        from_up = jnp.where((row_id == 0) & (r == 0), zero, from_up)
        from_left = jnp.where((lane_id == 0) & (c == 0), zero, from_left)
        grad_tv = from_up + from_left - (flow_down + flow_side)[8 : T + 8, :T]
        length = (squared * inverse)[8 : T + 8, :T]

        def spread(k):
            for i in range(0, T, CH):
                parts = []
                for at in (slice(i, i + CH), slice(T + i, T + i + CH)):
                    m_r, m_i = m_ref[0, at], m_ref[1, at]
                    m_r, m_i = lanes(m_r, m_r), lanes(m_i, m_i)
                    h_r, h_i = hr_ref[k, at], hi_ref[k, at]
                    parts.append((m_r * h_r + m_i * h_i, m_i * h_r - m_r * h_i))
                for j in range(2):
                    at = slice(j * T + i, j * T + i + CH)
                    b_ref[k, 0, at], b_ref[k, 1, at] = split(parts[0][j] + parts[1][j])
                    b_ref[k, 2, at], b_ref[k, 3, at] = split(parts[0][j] - parts[1][j])

        def along_rows(k):
            for n, name in enumerate(("even", "odd")):
                bh, bl = b_ref[k, 2 * n], b_ref[k, 2 * n + 1]
                z = mm(lanes(tab(name + "h"), tab(name + "h"), tab(name + "l")), rows(bh, bl, bh))
                for j in range(2):
                    at = j * T + n * R
                    part = slice(j * T, (j + 1) * T)
                    zh, zl = split(lanes(z[:R, part], z[R:, part]))
                    z_ref[k, at : at + R], z_ref[k, N + at : N + at + R] = zh, zl

        def along_lanes(k, total):
            wi = lanes(tab("wih")[:, :T], tab("wil")[:, :T])
            e = mm(z_ref[k], wi)
            e = (e[:N, :T] + e[:N, T:]) + (e[N:, :T] + e[N:, T:])
            field_ref[k] = e
            square = e * e
            return total + (square[:T] + square[T:])

        intensity = zero
        for step in range(K + 2):
            if 1 <= step <= K:
                along_rows(step - 1)
            if step < K:
                spread(step)
            if step >= 2:
                intensity = along_lanes(step - 2, intensity)
        wanted = rows(target_ref[pl.ds(0, R, stride=2), :], target_ref[pl.ds(1, R, stride=2), :])
        resist = 1.0 / (1.0 + jnp.exp(-SLOPE * (intensity - LEVEL)))
        miss = resist - wanted
        weight = 2.0 * miss * SLOPE * resist * (1.0 - resist)
        term = miss * miss + TV_WEIGHT * length + L1_WEIGHT * jnp.abs(point)
        goal_part[t] = jnp.sum(term.reshape(T // 8, 8, T), axis=0)

        gr_ref[...] = jnp.zeros_like(gr_ref)
        gi_ref[...] = jnp.zeros_like(gi_ref)
        def weigh(k):
            for j in range(2):
                for i in range(0, T, CH):
                    at = slice(j * T + i, j * T + i + CH)
                    v_ref[k, at, :T], v_ref[k, at, T:] = split(weight[i : i + CH] * field_ref[k, at])

        def from_lanes(k):
            wh, wl = tab("wh")[:T], tab("wl")[:T]
            v = v_ref[k]
            y = mm(lanes(v, v), rows(wh, wh, wl, wl))
            for n in range(2):
                for j in range(2):
                    part = slice(j * T, (j + 1) * T)
                    yh, yl = split(lanes(y[n * R : (n + 1) * R, part], y[T + n * R : T + (n + 1) * R, part]))
                    at = j * R
                    y_ref[k, n, at : at + R], y_ref[k, n, T + at : T + at + R] = yh, yl

        def gather(k):
            out = []
            for n in range(2):
                y2 = y_ref[k, n]
                bh = tab("bothh")[:, n * T : (n + 1) * T]
                bl = tab("bothl")[:, n * T : (n + 1) * T]
                out.append(mm(lanes(bh, bh, bl, bl), rows(y2, y2)))
            even, odd = out
            for i in range(0, T, CH):
                parts = [(x[i : i + CH], x[T + i : T + i + CH]) for x in (even, odd)]
                for n, sign in enumerate((1, -1)):
                    at = slice(n * T + i, n * T + i + CH)
                    s_r, s_i = (e + o if sign > 0 else e - o for e, o in zip(*parts))
                    h_r, h_i = hr_ref[k, at], hi_ref[k, at]
                    gr_ref[at] += h_r * s_r - h_i * s_i
                    gi_ref[at] += h_r * s_i + h_i * s_r

        last = t == ITERS - 1
        reducing = None
        if last:
            parts = [jnp.sum(goal_part[n], axis=0, keepdims=True) for n in range(ITERS)]
            parts = [part + pltpu.roll(part, R, 1) for part in parts]
            value = jnp.where(first_lanes[:1], parts[0], parts[1])
            reducing = reduce_start(0, value)
            pending += reducing
        for step in range(K + 2):
            if 1 <= step <= K:
                from_lanes(step - 1)
            if step < K:
                weigh(step)
            if step >= 2:
                gather(step - 2)
        g = lanes(gr_ref[:, :T] + gr_ref[:, T:], gi_ref[:, :T] + gi_ref[:, T:])
        gh, gl = split(g)

        def back(at):
            dh, dl = (rows(tab(name)[at : at + T], tab(name)[N + at : N + at + T]) for name in ("dh", "dl"))
            q = mm(lanes(dh, dh, dl), rows(gh, gl, gh))
            zh, zl = split(lanes(q[:T, :T] - q[T:, T:], q[:T, T:] + q[T:, :T]))
            return mm(lanes(zh, zh, zl), rows(tab("wih"), tab("wil"), tab("wih")))

        slot = 2 * t + 1
        halo = back(T)
        sent_corners = send_corners(slot, -1, halo[:, T:])
        own_ref[t] = halo[:, :T]
        sent = send_beyond(slot, -1, own_ref.at[t])
        g = back(0)
        sent += send_beside(slot, -1, g[:, T:])
        pending += sent_corners + sent
        if last:
            reducing = reduce_start(1, reduce_end(0, reducing))
            pending += reducing
        rows_live = jnp.where(upper, has_up.astype(F32), has_down.astype(F32))
        lanes_live = jnp.where(first_lanes, has_left.astype(F32), has_right.astype(F32))
        below, beside = arrived(slot, sent)
        grad_data = g[:, :T] + below * rows_live + beside * lanes_live
        corner = arrived_corners(slot, sent_corners)
        grad_data = 2.0 * (grad_data + corner * (rows_live * lanes_live))
        updated = jnp.clip(
            point - STEP_SIZE * (grad_data + TV_WEIGHT * grad_tv) - STEP_SIZE * L1_WEIGHT, 0.0, 1.0
        )
        if last:
            next_ref[...] = updated
            put(0, next_ref, next_hbm)
            total = reduce_end(1, reducing)
            scale = 1.0 / (size_r * size_c * T * T)
            for n in range(ITERS):
                goal_ref[n] = jnp.sum(jnp.where((lane_id[:1] < R) == (n == 0), total, 0.0)) * scale
        else:
            last_ref[...] = updated
            put(1, last_ref, last_hbm)
            point = extrapolate(t + 1, updated, previous)
            previous = updated
            sent = send_point(t + 1, point)
            pending += sent[0] + sent[1]
    for copy in pending:
        copy.wait_send()
    for copy in stored:
        copy.wait()


def shards(size_r, size_c, mask, mask_prev, target, kernels, restart):
    anywhere = pl.BlockSpec(memory_space=pltpu.HBM)
    rows_by, cols_by = factors(size_r, size_c)
    widest = max(rows_by[1] * cols_by[1], rows_by[0] * cols_by[0] * rows_by[2])
    results = pl.pallas_call(
        functools.partial(kernel, size_r, size_c),
        out_shape=(
            jax.ShapeDtypeStruct((T, T), F32),
            jax.ShapeDtypeStruct((T, T), F32),
            jax.ShapeDtypeStruct((ITERS,), F32),
        ),
        in_specs=[anywhere] * 6,
        out_specs=(anywhere, anywhere, pl.BlockSpec(memory_space=pltpu.SMEM)),
        scratch_shapes=[
            pltpu.VMEM((T, T), F32),
            pltpu.VMEM((T, T), F32),
            pltpu.VMEM((T, T), F32),
            pltpu.VMEM((T, T), F32),
            pltpu.VMEM((T, T), F32),
            pltpu.SMEM((1, 1, ITERS), jnp.int32),
            pltpu.VMEM((K, KS, 2, KS), F32),
            pltpu.VMEM(TABLE.shape, BF16),
            pltpu.VMEM((2, KP, N), F32),
            pltpu.VMEM((K, N, N), F32),
            pltpu.VMEM((K, N, N), F32),
            pltpu.VMEM((K, N, T), F32),
            pltpu.VMEM((N, N), F32),
            pltpu.VMEM((N, N), F32),
            pltpu.VMEM((ITERS, T, T), F32),
            pltpu.VMEM((ITERS, T, T), F32),
            pltpu.VMEM((K, 4, N, N), BF16),
            pltpu.VMEM((K, 2 * N, N), BF16),
            pltpu.VMEM((K, N, N), BF16),
            pltpu.VMEM((K, 2, N, N), BF16),
            pltpu.VMEM((2, N, T), F32),
            pltpu.VMEM((2 * ITERS, T, T), F32),
            pltpu.VMEM((2 * ITERS, 2, R, T), F32),
            pltpu.VMEM((2 * ITERS, 2, 2, R // 2, T), F32),
            pltpu.VMEM((2 * ITERS, 2, R, T), F32),
            pltpu.VMEM((2 * ITERS, 2, 2, R // 2, T), F32),
            pltpu.VMEM((ITERS, 8, T), F32),
            pltpu.VMEM((2, widest, 1, T), F32),
            pltpu.VMEM((2, 1, T), F32),
            pltpu.SemaphoreType.DMA((8,)),
            pltpu.SemaphoreType.DMA((2 * ITERS, 8)),
            pltpu.SemaphoreType.DMA((2 * ITERS, 8)),
            pltpu.SemaphoreType.DMA((2, widest)),
            pltpu.SemaphoreType.DMA((2, widest)),
        ],
        compiler_params=pltpu.CompilerParams(
            collective_id=0, has_side_effects=True, vmem_limit_bytes=62 * 1024 * 1024
        ),
        name="fista",
    )(mask, mask_prev, target, jnp.transpose(restart, (1, 2, 0)), jnp.transpose(kernels, (0, 2, 1, 3)), jnp.asarray(TABLE))
    return pl.pallas_call(
        store,
        out_shape=tuple(jax.ShapeDtypeStruct(x.shape, x.dtype) for x in results),
        in_specs=[anywhere] * 3,
        out_specs=(anywhere,) * 3,
        scratch_shapes=[
            pltpu.VMEM((T, T), F32),
            pltpu.VMEM((T, T), F32),
            pltpu.VMEM((ITERS,), F32),
            pltpu.SemaphoreType.DMA((2, 3)),
        ],
        name="store",
    )(*results)


def store(a_hbm, b_hbm, c_hbm, next_hbm, last_hbm, goal_hbm, a_ref, b_ref, c_ref, sems):
    trips = ((a_hbm, a_ref, next_hbm), (b_hbm, b_ref, last_hbm), (c_hbm, c_ref, goal_hbm))
    there = [pltpu.make_async_copy(x, y, sems.at[0, n]) for n, (x, y, _) in enumerate(trips)]
    back = [pltpu.make_async_copy(y, z, sems.at[1, n]) for n, (_, y, z) in enumerate(trips)]
    for copy in there:
        copy.start()
    for first, second in zip(there, back):
        first.wait()
        second.start()
    for copy in back:
        copy.wait()


def solution(mesh):
    in_specs = (P("row", "col"), P("row", "col"), P("row", "col"), P(), P(None, "row", "col"))
    out_specs = (P("row", "col"), P("row", "col"), P())
    body = functools.partial(shards, mesh.shape["row"], mesh.shape["col"])
    return jax.shard_map(body, mesh=mesh, in_specs=in_specs, out_specs=out_specs, check_vma=False)
```
